128 devices in a mesh: dp: 4 (over y_hi, core), vocab: 32 (over x, y_lo, z).
Axes of the slice: x: 4, y: 4 (y_hi: 2, y_lo: 2; y = y_hi * 2 + y_lo), z: 4, core: 2. Of those that a mesh axis runs over, the one named last changes fastest.
Arguments:
- hidden: bfloat16 [256, 7168], P(('dp', 'vocab')), may hold values from -82 to 82
- head_weight: bfloat16 [7168, 98304], P(None, ('dp', 'vocab')), may hold values from -4 to 4
- ref_logprobs: bfloat16 [256, 98304], P(('dp', 'vocab')), may hold values from -16 to -6
- token_ids: int32 [256], replicated, may hold values from 0 to 98303
- response_mask: int32 [256], replicated, may hold values 0 or 1
- advantages: float32 [256], replicated, may hold values from -0.6 to 0.6
Outputs:
- grad_hidden: bfloat16 [256, 7168], P(('dp', 'vocab'))
- grad_head: bfloat16 [7168, 98304], P(None, ('dp', 'vocab'))
The draws below stay inside these ranges and needn't reach their ends.
All inputs are finite; a program needn't handle non-finite values.
Results may differ from the reference program's by a relative error of at most 0.009.
Values may be sent and summed in bfloat16 or wider, within the bound.
No kernel may reach another device: no remote copies, remote signals or barrier semaphores. Data moves between devices by JAX's collectives and lax.ppermute only.
A program may use at most 128 MiB of HBM per device.

```python
import math
import jax
import jax.numpy as jnp
from jax import lax

D = 7168
TOKENS = 256
VOCAB = 98304


def weight_columns(key):
    base = jax.random.normal(jax.random.fold_in(key, 101), (D, VOCAB), jnp.float32)
    spread = jnp.exp(jax.random.uniform(jax.random.fold_in(key, 102), (VOCAB,), jnp.float32, math.log(0.5), math.log(3.0)))
    common = jax.random.normal(jax.random.fold_in(key, 103), (D,), jnp.float32) * (1.5 / math.sqrt(D))
    weight = base * (spread / math.sqrt(D))[None, :] + common[:, None]
    return (weight, common)


def draw_head_weight(key, part):
    weight, common = weight_columns(key)
    return weight.astype(jnp.bfloat16)


def sharp_values(weight, common, top_cols, levels):
    columns = weight[:, top_cols].T
    unit = common / jnp.sqrt(jnp.sum(common * common))
    along = jnp.sum(columns * unit[None, :], axis=1, keepdims=True)
    across = columns - along * unit[None, :]
    return levels * across / jnp.sum(across * across, axis=1, keepdims=True)


def draw_hidden(key, part):
    weight, common = weight_columns(key)
    key = jax.random.fold_in(key, 7)
    keys = jax.random.split(key, 8)
    row_scale = jnp.exp(jax.random.uniform(keys[0], (TOKENS, 1), jnp.float32, 0.0, math.log(6.0)))
    order = jax.random.permutation(keys[3], TOKENS)
    sharp_count = TOKENS // 4
    sharp_rows = order[4:4 + sharp_count]
    top_cols = jax.random.randint(keys[6], (sharp_count,), 0, VOCAB)
    levels = math.log(VOCAB) + jax.random.uniform(keys[7], (sharp_count, 1), jnp.float32, 4.5, 6.0)
    sharp = sharp_values(weight, common, top_cols, levels)
    values = jax.random.normal(keys[1], (TOKENS, D), jnp.float32) * row_scale
    values = values.at[sharp_rows].set(sharp)
    return values.astype(jnp.bfloat16)


def with_ends(values, key, smallest, largest):
    dims = values.shape
    index_at = [jax.random.randint(jax.random.fold_in(key, axis), (), 0, dims[axis]) for axis in range(len(dims))]
    values = values.at[tuple(index_at)].set(smallest)
    longest = dims.index(max(dims))
    index_at[longest] = (index_at[longest] + 1) % dims[longest]
    return values.at[tuple(index_at)].set(largest)


def shard_levels(rng, dims, shards, least, top_value):
    gain = 1.0
    for dim, parts in shards:
        heights = jax.random.uniform(jax.random.fold_in(jax.random.fold_in(rng, 6), dim), (parts,), jnp.float32, least / len(shards), top_value / len(shards))
        gain = gain * jnp.repeat(jnp.exp(heights), dims[dim] // parts).reshape((-1,) + (1,) * (len(dims) - 1 - dim))
    return gain


def scatter_about(key, extent, deviation, bound, kind=jnp.bfloat16):
    return jnp.clip(deviation * jax.random.normal(key, extent, jnp.float32), -bound, bound).astype(kind)


def setup_inputs(seed: int = 0) -> dict:
    key_list = jax.random.split(jax.random.key(seed), 7)
    return {
        "hidden": draw_hidden(jax.random.fold_in(key_list[6], 71), 0),
        "head_weight": draw_head_weight(jax.random.fold_in(key_list[6], 71), 0),
        "ref_logprobs": jnp.clip(-16.0 + 10.0 * jax.random.uniform(key_list[2], (TOKENS, VOCAB), jnp.float32) ** shard_levels(key_list[2], (TOKENS, VOCAB), ((0, 128),), -0.2, 0.2), -16.0, -6.0).astype(jnp.bfloat16),
        "token_ids": with_ends(jax.random.randint(key_list[3], (TOKENS,), 0, VOCAB), jax.random.fold_in(key_list[3], 1), 0, VOCAB - 1).astype(jnp.int32),
        "response_mask": with_ends((jax.random.randint(key_list[4], (TOKENS,), 0, 4) < 3).astype(jnp.int32), jax.random.fold_in(key_list[4], 1), 0, 1),
        "advantages": scatter_about(key_list[5], (TOKENS,), 0.1, 0.6, jnp.float32),
    }


grad_scale = 256.0


def reference(hidden, head_weight, ref_logprobs, token_ids, response_mask, advantages):
    logits = jnp.dot(hidden, head_weight, preferred_element_type=jnp.float32)
    row_top = jnp.max(logits, axis=1)
    shifted = logits - row_top[:, None]
    ref_values = ref_logprobs.astype(jnp.float32)
    scaled = jnp.exp(shifted)
    row_total = jnp.sum(scaled, axis=1)
    row_cross = jnp.sum(scaled * (shifted - ref_values), axis=1)
    log_total = jnp.log(row_total)
    divergence = row_cross / row_total - log_total
    log_probs = shifted - log_total[:, None]
    chance = jnp.exp(log_probs)
    chosen = (token_ids[:, None] == jnp.arange(VOCAB, dtype=jnp.int32)[None, :]).astype(jnp.float32)
    weighting = grad_scale * response_mask.astype(jnp.float32)
    grad_logits = (weighting[:, None] * (chance * (log_probs - ref_values - divergence[:, None])
                                         - advantages[:, None] * (chosen - chance))).astype(jnp.bfloat16)
    grad_head = lax.dot_general(hidden, grad_logits, (((0,), (0,)), ((), ())),
                                preferred_element_type=jnp.float32).astype(jnp.bfloat16)
    grad_hidden = lax.dot_general(grad_logits, head_weight, (((1,), (1,)), ((), ())),
                                  preferred_element_type=jnp.float32).astype(jnp.bfloat16)
    return grad_hidden, grad_head
```

```python
import functools

import jax
import jax.numpy as jnp
import numpy as np
from jax import lax
from jax.experimental import pallas as pl
from jax.experimental.pallas import tpu as pltpu
from jax.sharding import Mesh
from jax.sharding import PartitionSpec as P

grad_scale = 256.0

AXES = ("yh", "core", "x", "yl", "z")
SIZES = (2, 2, 4, 2, 4)
PEERS = 8
ROWS = 2
HALF = 128
MIB = 1 << 20


def device_at(x, y, z, core):
    return int(np.ravel_multi_index((y // 2, core, x, y % 2, z), SIZES))


PLACE = {(0, 0): 0, (1, 0): 1, (1, 1): 2, (0, 1): 3}


def chip(e, f):
    return tuple(PLACE[(e >> k) & 1, (f >> k) & 1] for k in (2, 1, 0))


def device(core, first, second):
    return device_at(*(chip(first, second) if core == 0 else chip(second, first)), core)


FIRST = [[device(c, v, s) for v in range(8)] for c in (0, 1) for s in range(8)]
SECOND = [[device(c, s, v) for v in range(8)] for c in (0, 1) for s in range(8)]
ORDER = np.array(
    [ROWS * device(c, first, second) + r for c in (0, 1) for second in range(8) for first in range(8) for r in range(ROWS)],
    np.int32,
)


def slots(core):
    out = []
    for first in range(8):
        for second in range(8):
            e, f = (first, second) if core == 0 else (second, first)
            out += [device_at(*chip(e, f), c) for c in (0, 1)]
    return out


SLOTS = np.array([slots(0), slots(1)], np.int32)


def exchange(x, groups):
    return lax.all_to_all(
        x, AXES, split_axis=0, concat_axis=0, axis_index_groups=groups, tiled=True
    )


def swap_cores(x):
    return lax.ppermute(x, "core", [(0, 1), (1, 0)])


def pack_kernel(columns, slot_ref, hidden_ref, ref_ref, out_ref):
    per_peer = 2 * PEERS

    def one(s, _):
        source = pl.multiple_of(slot_ref[s] * columns, 128)
        target = pl.multiple_of((s % per_peer) * columns, 128)
        out_ref[s // per_peer, :, pl.ds(target, columns)] = ref_ref[:, pl.ds(source, columns)]
        return 0

    lax.fori_loop(0, PEERS * per_peer, one, 0)
    rows = hidden_ref[...]
    for peer in range(PEERS):
        out_ref[peer, :, per_peer * columns :] = rows


def pack(slot, hidden, ref_logprobs, columns):
    width = 2 * PEERS * columns + hidden.shape[1]
    return pl.pallas_call(
        functools.partial(pack_kernel, columns),
        out_shape=jax.ShapeDtypeStruct((PEERS, ROWS, width), hidden.dtype),
        grid_spec=pltpu.PrefetchScalarGridSpec(
            num_scalar_prefetch=1,
            grid=(1,),
            in_specs=[
                pl.BlockSpec(hidden.shape, lambda i, s: (0, 0)),
                pl.BlockSpec(ref_logprobs.shape, lambda i, s: (0, 0)),
            ],
            out_specs=pl.BlockSpec((PEERS, ROWS, width), lambda i, s: (0, 0, 0)),
        ),
        compiler_params=pltpu.CompilerParams(vmem_limit_bytes=16 * MIB),
        name="pack",
    )(slot, hidden, ref_logprobs)


def logits_kernel(steps, core_ref, own_ref, other_ref, own_lp_ref, other_lp_ref, weight_ref, logits_ref, stats_ref):
    step = pl.program_id(0)
    weight = weight_ref[...]

    for side, x_ref in enumerate((own_ref, other_ref)):
        part = jnp.dot(x_ref[...], weight, preferred_element_type=jnp.float32)
        rows = pl.ds(side * HALF, HALF)

        @pl.when(step == 0)
        def _(part=part, rows=rows):
            logits_ref[rows, :] = part

        @pl.when(step > 0)
        def _(part=part, rows=rows):
            logits_ref[rows, :] += part

    @pl.when(step == steps - 1)
    def _():
        sides = []
        for side, lp_ref in enumerate((own_lp_ref, other_lp_ref)):
            logits = logits_ref[pl.ds(side * HALF, HALF), :]
            top = jnp.max(logits, axis=1, keepdims=True)
            shifted = logits - top
            scaled = jnp.exp(shifted)
            total = jnp.sum(scaled, axis=1, keepdims=True)
            cross = jnp.sum(scaled * (shifted - lp_ref[...].astype(jnp.float32)), axis=1, keepdims=True)
            lane = lax.broadcasted_iota(jnp.int32, (HALF, HALF), 1)
            table = jnp.where(lane == 0, top, jnp.where(lane == 1, total, cross))
            sides.append(table.T[:8, :])
        stats_ref[...] = jnp.concatenate(sides, axis=1)


def local_logits(core, own, other, weight, block=512):
    depth, columns = weight.shape
    first = 2 * columns // block
    steps = depth // block
    tokens = 2 * HALF
    x_spec = pl.BlockSpec((HALF, block), lambda k, c: (0, first + k))
    lp_spec = pl.BlockSpec((HALF, columns), lambda k, c: (0, c[0]))
    return pl.pallas_call(
        functools.partial(logits_kernel, steps),
        out_shape=(
            jax.ShapeDtypeStruct((tokens, columns), jnp.float32),
            jax.ShapeDtypeStruct((8, tokens), jnp.float32),
        ),
        grid_spec=pltpu.PrefetchScalarGridSpec(
            num_scalar_prefetch=1,
            grid=(steps,),
            in_specs=[x_spec, x_spec, lp_spec, lp_spec, pl.BlockSpec((block, columns), lambda k, c: (k, 0))],
            out_specs=(
                pl.BlockSpec((tokens, columns), lambda k, c: (0, 0)),
                pl.BlockSpec((8, tokens), lambda k, c: (0, 0)),
            ),
        ),
        compiler_params=pltpu.CompilerParams(vmem_limit_bytes=24 * MIB),
        cost_estimate=pl.CostEstimate(
            flops=2 * tokens * depth * columns, bytes_accessed=2 * depth * (columns + tokens), transcendentals=0
        ),
        name="logits",
    )(core, own, other, own, other, weight)


def hidden_grad_kernel(core_ref, logits_ref, own_lp_ref, other_lp_ref, token_ref, weight_ref, grad_ref, own_ref, other_ref):
    @pl.when(pl.program_id(0) == 0)
    def _():
        for side, lp_ref in enumerate((own_lp_ref, other_lp_ref)):
            rows = pl.ds(side * HALF, HALF)
            pad = jnp.zeros((HALF - 8, HALF), jnp.float32)
            table = jnp.concatenate([token_ref[:, side * HALF : (side + 1) * HALF], pad], axis=0).T
            top, log_total, divergence, advantage, weighting, chosen = (table[:, i : i + 1] for i in range(6))
            log_probs = (logits_ref[rows, :] - top) - log_total
            chance = jnp.exp(log_probs)
            entry = lax.broadcasted_iota(jnp.int32, log_probs.shape, 1).astype(jnp.float32)
            picked = jnp.where(entry == chosen, 1.0, 0.0)
            ref_values = lp_ref[...].astype(jnp.float32)
            grad = weighting * (chance * (log_probs - ref_values - divergence) - advantage * (picked - chance))
            grad_ref[rows, :] = grad.astype(grad_ref.dtype)

    out = lax.dot_general(
        grad_ref[...], weight_ref[...], (((1,), (1,)), ((), ())), preferred_element_type=jnp.float32
    )
    own_ref[...] = out[:HALF]
    other_ref[...] = out[HALF:].astype(other_ref.dtype)


def hidden_grad(core, logits, own, other, token, weight, block=1024):
    depth, columns = weight.shape
    tokens = logits.shape[0]
    lp_spec = pl.BlockSpec((HALF, columns), lambda k, c: (0, c[0]))
    whole = lambda shape: pl.BlockSpec(shape, lambda k, c: (0, 0))
    return pl.pallas_call(
        hidden_grad_kernel,
        out_shape=(
            jax.ShapeDtypeStruct((tokens, columns), weight.dtype),
            jax.ShapeDtypeStruct((HALF, depth), jnp.float32),
            jax.ShapeDtypeStruct((HALF, depth), weight.dtype),
        ),
        grid_spec=pltpu.PrefetchScalarGridSpec(
            num_scalar_prefetch=1,
            grid=(depth // block,),
            in_specs=[
                whole(logits.shape),
                lp_spec,
                lp_spec,
                whole(token.shape),
                pl.BlockSpec((block, columns), lambda k, c: (k, 0)),
            ],
            out_specs=(
                whole((tokens, columns)),
                pl.BlockSpec((HALF, block), lambda k, c: (0, k)),
                pl.BlockSpec((HALF, block), lambda k, c: (0, k)),
            ),
        ),
        compiler_params=pltpu.CompilerParams(vmem_limit_bytes=24 * MIB),
        cost_estimate=pl.CostEstimate(
            flops=2 * tokens * depth * columns, bytes_accessed=2 * depth * (columns + 3 * HALF), transcendentals=0
        ),
        name="hidden_grad",
    )(core, logits, own, other, token, weight)


def head_grad_kernel(own_ref, other_ref, grad_ref, out_ref):
    x = jnp.concatenate([own_ref[...], other_ref[...]], axis=0)
    out_ref[...] = lax.dot_general(
        x, grad_ref[...], (((0,), (0,)), ((), ())), preferred_element_type=jnp.float32
    ).astype(out_ref.dtype)


def head_grad(own, other, grad, depth, block=512):
    tokens, columns = grad.shape
    first = 2 * columns // block
    x_spec = pl.BlockSpec((HALF, block), lambda k: (0, first + k))
    return pl.pallas_call(
        head_grad_kernel,
        out_shape=jax.ShapeDtypeStruct((depth, columns), grad.dtype),
        grid=(depth // block,),
        in_specs=[x_spec, x_spec, pl.BlockSpec(grad.shape, lambda k: (0, 0))],
        out_specs=pl.BlockSpec((block, columns), lambda k: (k, 0)),
        compiler_params=pltpu.CompilerParams(vmem_limit_bytes=24 * MIB),
        cost_estimate=pl.CostEstimate(
            flops=2 * tokens * depth * columns, bytes_accessed=2 * depth * (columns + tokens), transcendentals=0
        ),
        name="head_grad",
    )(own, other, grad)


def local(hidden, head_weight, ref_logprobs, token_ids, response_mask, advantages):
    depth, columns = head_weight.shape
    core = lax.axis_index("core")
    core_arr = core.reshape(1).astype(jnp.int32)
    slot = jnp.where(core == 0, SLOTS[0], SLOTS[1])

    sent = pack(slot, hidden, ref_logprobs, columns)
    got = exchange(sent, FIRST).reshape(PEERS * ROWS, sent.shape[2])
    cut = 2 * PEERS * columns
    lp = got[:, :cut].reshape(PEERS * ROWS, PEERS, 2 * columns).transpose(1, 0, 2)
    rows = jnp.broadcast_to(got[None, :, cut:], (PEERS, PEERS * ROWS, depth))
    own = exchange(jnp.concatenate([lp, rows], axis=2), SECOND).reshape(HALF, 2 * columns + depth)
    other = swap_cores(own)

    logits, stats = local_logits(core_arr, own, other, head_weight)

    def turn(table):
        return jnp.where(core == 0, table, jnp.roll(table, HALF, axis=1))

    stats = turn(stats[:3]).reshape(1, 1, 3 * 2 * HALF)
    everyone = lax.all_to_all(
        jnp.broadcast_to(stats, (128,) + stats.shape[1:]), AXES, split_axis=0, concat_axis=0, tiled=True
    ).reshape(128, 3, 2 * HALF)
    tops, totals, crosses = everyone[:, 0], everyone[:, 1], everyone[:, 2]
    row_top = jnp.max(tops, axis=0)
    below = tops - row_top[None, :]
    factor = jnp.exp(below)
    row_total = jnp.sum(factor * totals, axis=0)
    row_cross = jnp.sum(factor * (crosses + below * totals), axis=0)
    log_total = jnp.log(row_total)
    divergence = row_cross / row_total - log_total

    first_entry = lax.axis_index(AXES) * columns
    chosen = (token_ids[ORDER] - first_entry).astype(jnp.float32)
    weighting = grad_scale * response_mask[ORDER].astype(jnp.float32)
    zero = jnp.zeros_like(row_top)
    token = turn(
        jnp.stack([row_top, log_total, divergence, advantages[ORDER], weighting, chosen, zero, zero])
    )

    grad, mine, theirs = hidden_grad(core_arr, logits, own, other, token, head_weight)
    grad_head = head_grad(own, other, grad, depth)

    part = (mine + swap_cores(theirs).astype(jnp.float32)).astype(hidden.dtype)
    part = exchange(part.reshape(PEERS, PEERS * ROWS, depth), SECOND)
    part = jnp.sum(part.astype(jnp.float32), axis=0).astype(hidden.dtype)
    part = exchange(part.reshape(PEERS, ROWS, depth), FIRST)
    grad_hidden = jnp.sum(part.astype(jnp.float32), axis=0).astype(hidden.dtype)
    return grad_hidden, grad_head


def solution(mesh):
    fine = Mesh(mesh.devices.reshape(SIZES), AXES)
    return jax.shard_map(
        local,
        mesh=fine,
        in_specs=(P(AXES, None), P(None, AXES), P(AXES, None), P(), P(), P()),
        out_specs=(P(AXES, None), P(None, AXES)),
        check_vma=False,
    )
```

```python
import functools

import jax
import jax.numpy as jnp
import numpy as np
from jax import lax
from jax.experimental import pallas as pl
from jax.experimental.pallas import tpu as pltpu
from jax.sharding import Mesh
from jax.sharding import PartitionSpec as P

grad_scale = 256.0

AXES = ("yh", "core", "x", "yl", "z")
CHIPS = ("yh", "x", "yl", "z")
SIZES = (2, 2, 4, 2, 4)
PEERS = 8
ROWS = 2
HALF = 128
MIB = 1 << 20


def device_at(x, y, z, core):
    return int(np.ravel_multi_index((y // 2, core, x, y % 2, z), SIZES))


PLACE = {(0, 0): 0, (1, 0): 1, (1, 1): 2, (0, 1): 3}


def chip(e, f):
    return tuple(PLACE[(e >> k) & 1, (f >> k) & 1] for k in (2, 1, 0))


def device(core, first, second, to=None):
    place = chip(first, second) if core == 0 else chip(second, first)
    return device_at(*place, core if to is None else to)


FIRST = [[device(c, v, s) for v in range(8)] for c in (0, 1) for s in range(8)]
SECOND = [[device(c, s, v) for v in range(8)] for c in (0, 1) for s in range(8)]
ORDER = [
    [ROWS * device(c, first, second) + r for second in range(8) for first in range(8) for r in range(ROWS)]
    for c in (0, 1)
]
LOCAL_ORDER = np.array([ORDER[0] + ORDER[1], ORDER[1] + ORDER[0]], np.int32)


def exchange(x, groups):
    return lax.all_to_all(
        x, AXES, split_axis=0, concat_axis=0, axis_index_groups=groups, tiled=True
    )


def swap_cores(x):
    return lax.ppermute(x, "core", [(0, 1), (1, 0)])


def pack_kernel(columns, hidden_ref, ref_ref, out_ref):
    core = lax.axis_index("core")
    for mine in (0, 1):

        @pl.when(core == mine)
        def _(mine=mine):
            for first in range(PEERS):
                target = 0
                for second in range(PEERS):
                    for to in (mine, 1 - mine):
                        source = device(mine, first, second, to) * columns
                        out_ref[first, :, target : target + columns] = ref_ref[:, source : source + columns]
                        target += columns

    rows = hidden_ref[...]
    for peer in range(PEERS):
        out_ref[peer, :, 2 * PEERS * columns :] = rows


def pack(hidden, ref_logprobs, columns):
    width = 2 * PEERS * columns + hidden.shape[1]
    whole = lambda shape: pl.BlockSpec(shape, lambda i: (0,) * len(shape))
    return pl.pallas_call(
        functools.partial(pack_kernel, columns),
        out_shape=jax.ShapeDtypeStruct((PEERS, ROWS, width), hidden.dtype),
        grid=(1,),
        in_specs=[whole(hidden.shape), whole(ref_logprobs.shape)],
        out_specs=whole((PEERS, ROWS, width)),
        compiler_params=pltpu.CompilerParams(vmem_limit_bytes=8 * MIB),
        name="pack",
    )(pltpu.with_memory_space_constraint(hidden, pltpu.HBM), pltpu.with_memory_space_constraint(ref_logprobs, pltpu.HBM))


def logits_kernel(block, first, own_ref, other_ref, weight_ref, logits_ref, stats_ref):
    depth, columns = weight_ref.shape
    for step in range(depth // block):
        here = slice(first + step * block, first + (step + 1) * block)
        x = jnp.concatenate([own_ref[:, here], other_ref[:, here]], axis=0)
        part = jnp.dot(x, weight_ref[step * block : (step + 1) * block, :], preferred_element_type=jnp.float32)
        if step == 0:
            logits_ref[...] = part
        else:
            logits_ref[...] += part
    rows = []
    for side, lp_ref in enumerate((own_ref, other_ref)):
        logits = logits_ref[side * HALF : (side + 1) * HALF, :]
        lp = lp_ref[:, side * columns : (side + 1) * columns].astype(jnp.float32)
        top = jnp.max(logits, axis=1, keepdims=True)
        shifted = logits - top
        scaled = jnp.exp(shifted)
        total = jnp.sum(scaled, axis=1, keepdims=True)
        cross = jnp.sum(scaled * (shifted - lp), axis=1, keepdims=True)
        lane = lax.broadcasted_iota(jnp.int32, (HALF, HALF), 1)
        rows.append(jnp.where(lane == 0, top, jnp.where(lane == 1, total, cross)).T)
    parts = [rows[side][i : i + 1] for i in range(3) for side in (0, 1)]
    stats_ref[...] = jnp.concatenate(parts + [jnp.zeros((2, HALF), jnp.float32)], axis=0)


def local_logits(own, other, weight, block=1024):
    depth, columns = weight.shape
    tokens = 2 * HALF
    return pl.pallas_call(
        functools.partial(logits_kernel, block, 2 * columns),
        out_shape=(
            jax.ShapeDtypeStruct((tokens, columns), jnp.float32),
            jax.ShapeDtypeStruct((8, HALF), jnp.float32),
        ),
        in_specs=[pl.BlockSpec(memory_space=pltpu.VMEM)] * 3,
        out_specs=(pl.BlockSpec(memory_space=pltpu.VMEM),) * 2,
        compiler_params=pltpu.CompilerParams(vmem_limit_bytes=24 * MIB),
        cost_estimate=pl.CostEstimate(
            flops=2 * tokens * depth * columns, bytes_accessed=2 * depth * (columns + tokens), transcendentals=0
        ),
        name="logits",
    )(own, other, weight)


def merged(tops, totals, crosses):
    top = jnp.max(tops, axis=0)
    below = tops - top[None]
    factor = jnp.exp(below)
    return top, jnp.sum(factor * totals, axis=0), jnp.sum(factor * (crosses + below * totals), axis=0)


def merge_kernel(mine_ref, theirs_ref, out_ref):
    mine, theirs = mine_ref[...], theirs_ref[...]
    pair = lambda i: jnp.stack(
        [mine[2 * i : 2 * i + 2], jnp.concatenate([theirs[2 * i + 1 : 2 * i + 2], theirs[2 * i : 2 * i + 1]], axis=0)]
    )
    top, total, cross = merged(pair(0), pair(1), pair(2))
    tile = jnp.concatenate([top, total, cross, jnp.zeros_like(top)], axis=0)
    out_ref[...] = jnp.broadcast_to(tile[None], out_ref.shape)


def merge(mine, theirs, peers):
    return pl.pallas_call(
        merge_kernel,
        out_shape=jax.ShapeDtypeStruct((peers,) + mine.shape, mine.dtype),
        in_specs=[pl.BlockSpec(memory_space=pltpu.VMEM)] * 2,
        out_specs=pl.BlockSpec(memory_space=pltpu.VMEM),
        compiler_params=pltpu.CompilerParams(vmem_limit_bytes=8 * MIB),
        name="merge",
    )(mine, theirs)


def hidden_grad_kernel(block, logits_ref, own_ref, other_ref, stats_ref, token_ref, weight_ref, grad_ref, mine_ref, theirs_ref):
    depth, columns = weight_ref.shape
    stats = stats_ref[...]
    top, total, cross = merged(stats[:, 0:2], stats[:, 2:4], stats[:, 4:6])
    log_total = jnp.log(total)
    divergence = cross / total - log_total
    for side, lp_ref in enumerate((own_ref, other_ref)):
        rows = slice(side * HALF, (side + 1) * HALF)
        lines = [v[side : side + 1] for v in (top, log_total, divergence)]
        lines += [token_ref[2 * i + side : 2 * i + side + 1, :] for i in range(3)]
        pad = jnp.zeros((HALF - len(lines), HALF), jnp.float32)
        table = jnp.concatenate(lines + [pad], axis=0).T
        row_top, row_log, row_div, chosen, weighting, advantage = (table[:, i : i + 1] for i in range(6))
        log_probs = (logits_ref[rows, :] - row_top) - row_log
        chance = jnp.exp(log_probs)
        entry = lax.broadcasted_iota(jnp.int32, log_probs.shape, 1).astype(jnp.float32)
        picked = jnp.where(entry == chosen, 1.0, 0.0)
        lp = lp_ref[:, side * columns : (side + 1) * columns].astype(jnp.float32)
        grad = weighting * (chance * (log_probs - lp - row_div) - advantage * (picked - chance))
        grad_ref[rows, :] = grad.astype(grad_ref.dtype)

    for step in range(depth // block):
        here = slice(step * block, (step + 1) * block)
        out = lax.dot_general(
            grad_ref[...], weight_ref[here, :], (((1,), (1,)), ((), ())), preferred_element_type=jnp.float32
        )
        mine_ref[:, here] = out[:HALF]
        theirs_ref[:, here] = out[HALF:].astype(theirs_ref.dtype)


def hidden_grad(logits, own, other, stats, token, weight, block=1024):
    depth, columns = weight.shape
    tokens = logits.shape[0]
    return pl.pallas_call(
        functools.partial(hidden_grad_kernel, block),
        out_shape=(
            jax.ShapeDtypeStruct((tokens, columns), weight.dtype),
            jax.ShapeDtypeStruct((HALF, depth), jnp.float32),
            jax.ShapeDtypeStruct((HALF, depth), weight.dtype),
        ),
        in_specs=[pl.BlockSpec(memory_space=pltpu.VMEM)] * 6,
        out_specs=(pl.BlockSpec(memory_space=pltpu.VMEM),) * 3,
        compiler_params=pltpu.CompilerParams(vmem_limit_bytes=28 * MIB),
        cost_estimate=pl.CostEstimate(
            flops=2 * tokens * depth * columns, bytes_accessed=2 * depth * (columns + 3 * HALF), transcendentals=0
        ),
        name="hidden_grad",
    )(logits, own, other, stats, token, weight)


def head_grad_kernel(own_ref, other_ref, grad_ref, out_ref):
    x = jnp.concatenate([own_ref[...], other_ref[...]], axis=0)
    out_ref[...] = lax.dot_general(
        x, grad_ref[...], (((0,), (0,)), ((), ())), preferred_element_type=jnp.float32
    ).astype(out_ref.dtype)


def head_grad(own, other, grad, depth, block=512):
    tokens, columns = grad.shape
    first = 2 * columns // block
    x_spec = pl.BlockSpec((HALF, block), lambda k: (0, first + k))
    return pl.pallas_call(
        head_grad_kernel,
        out_shape=jax.ShapeDtypeStruct((depth, columns), grad.dtype),
        grid=(depth // block,),
        in_specs=[x_spec, x_spec, pl.BlockSpec(grad.shape, lambda k: (0, 0))],
        out_specs=pl.BlockSpec((block, columns), lambda k: (k, 0)),
        compiler_params=pltpu.CompilerParams(vmem_limit_bytes=16 * MIB),
        cost_estimate=pl.CostEstimate(
            flops=2 * tokens * depth * columns, bytes_accessed=2 * depth * (columns + tokens), transcendentals=0
        ),
        name="head_grad",
    )(own, other, grad)


def local(hidden, head_weight, ref_logprobs, token_ids, response_mask, advantages):
    depth, columns = head_weight.shape
    core = lax.axis_index("core")
    weight = pltpu.with_memory_space_constraint(head_weight, pltpu.VMEM)

    order = jnp.where(core == 0, LOCAL_ORDER[0], LOCAL_ORDER[1])
    places = lax.broadcasted_iota(jnp.int32, (2 * HALF, 2 * HALF), 0)
    arrange = lambda v: jnp.sum(jnp.where(places == order[None, :], v[:, None], 0), axis=0)
    chosen = (arrange(token_ids) - lax.axis_index(AXES) * columns).astype(jnp.float32)
    weighting = grad_scale * arrange(response_mask).astype(jnp.float32)
    token = jnp.concatenate([chosen, weighting, arrange(advantages), jnp.zeros_like(chosen)]).reshape(8, HALF)

    sent, token = lax.optimization_barrier((pack(hidden, ref_logprobs, columns), token))
    got = exchange(sent, FIRST).reshape(PEERS * ROWS, sent.shape[2])
    cut = 2 * PEERS * columns
    lp = got[:, :cut].reshape(PEERS * ROWS, PEERS, 2 * columns).transpose(1, 0, 2)
    rows = jnp.broadcast_to(got[None, :, cut:], (PEERS, PEERS * ROWS, depth))
    own = exchange(jnp.concatenate([lp, rows], axis=2), SECOND).reshape(HALF, 2 * columns + depth)
    other = swap_cores(own)

    logits, stats = local_logits(own, other, weight)
    stats = merge(stats, swap_cores(stats), 64)
    stats = lax.all_to_all(stats, CHIPS, split_axis=0, concat_axis=0, tiled=True)

    grad, mine, theirs = hidden_grad(logits, own, other, stats, token, weight)
    grad_head = head_grad(own, other, grad, depth)

    part = (mine + swap_cores(theirs).astype(jnp.float32)).astype(hidden.dtype)
    part = exchange(part.reshape(PEERS, PEERS * ROWS, depth), SECOND)
    part = jnp.sum(part.astype(jnp.float32), axis=0).astype(hidden.dtype)
    part, grad_head = lax.optimization_barrier((part.reshape(PEERS, ROWS, depth), grad_head))
    part = exchange(part, FIRST)
    grad_hidden = jnp.sum(part.astype(jnp.float32), axis=0).astype(hidden.dtype)
    return grad_hidden, grad_head


def solution(mesh):
    fine = Mesh(mesh.devices.reshape(SIZES), AXES)
    return jax.shard_map(
        local,
        mesh=fine,
        in_specs=(P(AXES, None), P(None, AXES), P(AXES, None), P(), P(), P()),
        out_specs=(P(AXES, None), P(None, AXES)),
        check_vma=False,
    )
```

```python
import functools

import jax
import jax.numpy as jnp
import numpy as np
from jax import lax
from jax.experimental import pallas as pl
from jax.experimental.pallas import tpu as pltpu
from jax.sharding import Mesh
from jax.sharding import PartitionSpec as P

grad_scale = 256.0

AXES = ("yh", "core", "x", "yl", "z")
CHIPS = ("yh", "x", "yl", "z")
SIZES = (2, 2, 4, 2, 4)
PEERS = 8
ROWS = 2
HALF = 128
MIB = 1 << 20


def device_at(x, y, z, core):
    return int(np.ravel_multi_index((y // 2, core, x, y % 2, z), SIZES))


PLACE = {(0, 0): 0, (1, 0): 1, (1, 1): 2, (0, 1): 3}


def chip(e, f):
    return tuple(PLACE[(e >> k) & 1, (f >> k) & 1] for k in (2, 1, 0))


def device(core, first, second, to=None):
    place = chip(first, second) if core == 0 else chip(second, first)
    return device_at(*place, core if to is None else to)


FIRST = [[device(c, v, s) for v in range(8)] for c in (0, 1) for s in range(8)]
SECOND = [[device(c, s, v) for v in range(8)] for c in (0, 1) for s in range(8)]
ORDER = [
    [ROWS * device(c, first, second) + r for second in range(8) for first in range(8) for r in range(ROWS)]
    for c in (0, 1)
]

def exchange(x, groups):
    return lax.all_to_all(
        x, AXES, split_axis=0, concat_axis=0, axis_index_groups=groups, tiled=True
    )


def swap_cores(x):
    return lax.ppermute(x, "core", [(0, 1), (1, 0)])


def pack_kernel(columns, hidden_ref, ref_ref, out_ref):
    core = lax.axis_index("core")
    for mine in (0, 1):

        @pl.when(core == mine)
        def _(mine=mine):
            for first in range(PEERS):
                target = 0
                for second in range(PEERS):
                    for to in (mine, 1 - mine):
                        source = device(mine, first, second, to) * columns
                        out_ref[first, :, target : target + columns] = ref_ref[:, source : source + columns]
                        target += columns

    rows = hidden_ref[...]
    for peer in range(PEERS):
        out_ref[peer, :, 2 * PEERS * columns :] = rows


def pack(hidden, ref_logprobs, columns):
    width = 2 * PEERS * columns + hidden.shape[1]
    whole = lambda shape: pl.BlockSpec(shape, lambda i: (0,) * len(shape))
    return pl.pallas_call(
        functools.partial(pack_kernel, columns),
        out_shape=jax.ShapeDtypeStruct((PEERS, ROWS, width), hidden.dtype),
        grid=(1,),
        in_specs=[whole(hidden.shape), whole(ref_logprobs.shape)],
        out_specs=whole((PEERS, ROWS, width)),
        compiler_params=pltpu.CompilerParams(vmem_limit_bytes=8 * MIB),
        name="pack",
    )(pltpu.with_memory_space_constraint(hidden, pltpu.HBM), pltpu.with_memory_space_constraint(ref_logprobs, pltpu.HBM))


def spread_kernel(columns, in_ref, rows_ref, lp_ref):
    depth = rows_ref.shape[1]
    first = in_ref.shape[2] - depth

    def rows(start, size):
        parts = [in_ref[peer, :, start : start + size].astype(jnp.float32) for peer in range(PEERS)]
        return jnp.concatenate(parts, axis=0).astype(rows_ref.dtype)

    block = 512
    for start in range(0, depth, block):
        rows_ref[:, start : start + block] = rows(first + start, block)
    for peer in range(PEERS):
        lp_ref[peer] = rows(peer * 2 * columns, 2 * columns)


def spread(got, depth, columns):
    vmem = pl.BlockSpec(memory_space=pltpu.VMEM)
    rows, lp = pl.pallas_call(
        functools.partial(spread_kernel, columns),
        out_shape=(
            jax.ShapeDtypeStruct((PEERS * ROWS, depth), got.dtype),
            jax.ShapeDtypeStruct((PEERS, PEERS * ROWS, 2 * columns), got.dtype),
        ),
        in_specs=[vmem],
        out_specs=(vmem, vmem),
        compiler_params=pltpu.CompilerParams(vmem_limit_bytes=8 * MIB),
        name="spread",
    )(got)
    rows = jnp.broadcast_to(rows[None], (PEERS,) + rows.shape)
    return jnp.concatenate([rows, lp], axis=2)


def token_order(core):
    place = lax.broadcasted_iota(jnp.int32, (1, HALF), 1)
    second, first, row = place >> 4, (place >> 1) & 7, place & 1
    e = jnp.where(core == 0, first, second)
    f = first + second - e
    low = e ^ f
    bit = lambda v, k: (v >> k) & 1
    index = bit(f, 1) * 2 + core
    index = index * 4 + 2 * bit(f, 2) + bit(low, 2)
    index = index * 2 + bit(low, 1)
    index = index * 4 + 2 * bit(f, 0) + bit(low, 0)
    return ROWS * index + row


def token_lines(columns, id_ref, mask_ref, advantage_ref):
    core = lax.axis_index("core")
    mine = lax.axis_index(AXES)
    other = mine + (1 - 2 * core) * (SIZES[2] * SIZES[3] * SIZES[4])
    tokens = id_ref.shape[1]
    lines = [
        id_ref[...].astype(jnp.float32),
        grad_scale * mask_ref[...].astype(jnp.float32),
        advantage_ref[...],
        jnp.zeros((HALF - 3, tokens), jnp.float32),
    ]
    table = jnp.concatenate(lines, axis=0).T
    here = lax.broadcasted_iota(jnp.int32, (tokens, HALF), 0) == token_order(core)
    ids, weighting, advantage = (
        jnp.sum(jnp.where(here, table[:, i : i + 1], 0.0), axis=0, keepdims=True) for i in range(3)
    )
    places = [ids - (d * columns).astype(jnp.float32) for d in (mine, other)]
    return jnp.concatenate(places + [weighting, advantage, jnp.zeros((4, HALF), jnp.float32)], axis=0)


def logits_kernel(
    block, own_ref, weight_ref, other_weight_ref, id_ref, mask_ref, advantage_ref, logits_ref, stats_ref, token_ref
):
    depth, columns = weight_ref.shape
    for side, w_ref in enumerate((weight_ref, other_weight_ref)):
        here = slice(side * columns, (side + 1) * columns)
        for step in range(depth // block):
            rows = slice(step * block, (step + 1) * block)
            part = jnp.dot(own_ref[:, rows], w_ref[rows, :], preferred_element_type=jnp.float32)
            if step == 0:
                logits_ref[:, here] = part
            else:
                logits_ref[:, here] += part
    token_ref[...] = token_lines(columns, id_ref, mask_ref, advantage_ref)
    logits = logits_ref[...]
    top = jnp.max(logits, axis=1, keepdims=True)
    shifted = logits - top
    scaled = jnp.exp(shifted)
    total = jnp.sum(scaled, axis=1, keepdims=True)
    cross = jnp.sum(scaled * (shifted - own_ref[:, depth:].astype(jnp.float32)), axis=1, keepdims=True)
    lane = lax.broadcasted_iota(jnp.int32, (HALF, HALF), 1)
    tile = jnp.where(lane == 0, top, jnp.where(lane == 1, total, cross)).T[:8]
    stats_ref[...] = jnp.broadcast_to(tile[None], stats_ref.shape)


def local_logits(own, weight, other_weight, tokens, peers, block=1024):
    depth, columns = weight.shape
    vmem = pl.BlockSpec(memory_space=pltpu.VMEM)
    return pl.pallas_call(
        functools.partial(logits_kernel, block),
        out_shape=(
            jax.ShapeDtypeStruct((HALF, 2 * columns), jnp.float32),
            jax.ShapeDtypeStruct((peers, 8, HALF), jnp.float32),
            jax.ShapeDtypeStruct((8, HALF), jnp.float32),
        ),
        in_specs=[vmem] * 6,
        out_specs=(vmem,) * 3,
        compiler_params=pltpu.CompilerParams(vmem_limit_bytes=16 * MIB),
        cost_estimate=pl.CostEstimate(
            flops=4 * HALF * depth * columns, bytes_accessed=4 * depth * columns, transcendentals=0
        ),
        name="logits",
    )(own, weight, other_weight, *(v.reshape(1, -1) for v in tokens))


def hidden_grad_kernel(
    block, logits_ref, own_ref, stats_ref, token_ref, weight_ref, other_weight_ref,
    grad_ref, other_grad_ref, out_ref, sums, sems,
):
    depth, columns = weight_ref.shape
    tops, totals, crosses = (stats_ref[:, i, :] for i in range(3))
    top = jnp.max(tops, axis=0, keepdims=True)
    below = tops - top
    factor = jnp.exp(below)
    total = jnp.sum(factor * totals, axis=0, keepdims=True)
    cross = jnp.sum(factor * (crosses + below * totals), axis=0, keepdims=True)
    log_total = jnp.log(total)
    divergence = cross / total - log_total
    lines = [top, log_total, divergence, token_ref[0:4, :], jnp.zeros((HALF - 7, HALF), jnp.float32)]
    table = jnp.concatenate(lines, axis=0).T
    row_top, row_log, row_div, place, other_place, weighting, advantage = (table[:, i : i + 1] for i in range(7))
    for side, (g_ref, chosen) in enumerate(((grad_ref, place), (other_grad_ref, other_place))):
        here = slice(side * columns, (side + 1) * columns)
        log_probs = (logits_ref[:, here] - row_top) - row_log
        chance = jnp.exp(log_probs)
        entry = lax.broadcasted_iota(jnp.int32, log_probs.shape, 1).astype(jnp.float32)
        picked = jnp.where(entry == chosen, 1.0, 0.0)
        lp = own_ref[:, depth + side * columns : depth + (side + 1) * columns].astype(jnp.float32)
        grad = weighting * (chance * (log_probs - lp - row_div) - advantage * (picked - chance))
        g_ref[...] = grad.astype(g_ref.dtype)

    def copy(step):
        here = pl.ds(step * block, block)
        return pltpu.make_async_copy(sums.at[:, here], out_ref.at[:, here], sems.at[step])

    for step in range(depth // block):
        here = slice(step * block, (step + 1) * block)
        total = [
            lax.dot_general(w_ref[here, :], g_ref[...], (((1,), (1,)), ((), ())), preferred_element_type=jnp.float32)
            for g_ref, w_ref in ((grad_ref, weight_ref), (other_grad_ref, other_weight_ref))
        ]
        sums[:, here] = (total[0] + total[1]).T.astype(sums.dtype)
        copy(step).start()
    for step in range(depth // block):
        copy(step).wait()


def hidden_grad(logits, own, stats, token, weight, other_weight, block=1024):
    depth, columns = weight.shape
    part = jax.ShapeDtypeStruct((HALF, columns), weight.dtype)
    return pl.pallas_call(
        functools.partial(hidden_grad_kernel, block),
        out_shape=(part, part, pltpu.HBM((HALF, depth), weight.dtype)),
        in_specs=[pl.BlockSpec(memory_space=pltpu.VMEM)] * 6,
        out_specs=(
            pl.BlockSpec(memory_space=pltpu.VMEM),
            pl.BlockSpec(memory_space=pltpu.VMEM),
            pl.BlockSpec(memory_space=pltpu.HBM),
        ),
        scratch_shapes=[pltpu.VMEM((HALF, depth), weight.dtype), pltpu.SemaphoreType.DMA((depth // block,))],
        compiler_params=pltpu.CompilerParams(vmem_limit_bytes=16 * MIB),
        cost_estimate=pl.CostEstimate(
            flops=8 * HALF * depth * columns, bytes_accessed=4 * depth * columns, transcendentals=0
        ),
        name="hidden_grad",
    )(logits, own, stats, token, weight, other_weight)


def sum_kernel(part_ref, out_ref, block=1024):
    depth = part_ref.shape[2]
    for start in range(0, depth, block):
        here = slice(start, start + block)
        parts = [part_ref[peer, :, here].astype(jnp.float32) for peer in range(PEERS)]
        while len(parts) > 1:
            parts = [a + b for a, b in zip(parts[::2], parts[1::2])]
        out_ref[:, here] = parts[0].astype(out_ref.dtype)


def add_up(parts):
    return pl.pallas_call(
        sum_kernel,
        out_shape=jax.ShapeDtypeStruct(parts.shape[1:], parts.dtype),
        in_specs=[pl.BlockSpec(memory_space=pltpu.VMEM)],
        out_specs=pl.BlockSpec(memory_space=pltpu.VMEM),
        compiler_params=pltpu.CompilerParams(vmem_limit_bytes=8 * MIB),
        name="add_up",
    )(pltpu.with_memory_space_constraint(parts, pltpu.VMEM))


def head_grad_kernel(own_ref, other_ref, own_grad_ref, other_grad_ref, out_ref):
    x = jnp.concatenate([own_ref[...], other_ref[...]], axis=0)
    grad = jnp.concatenate([own_grad_ref[...], other_grad_ref[...]], axis=0)
    out_ref[...] = lax.dot_general(
        x, grad, (((0,), (0,)), ((), ())), preferred_element_type=jnp.float32
    ).astype(out_ref.dtype)


def head_grad(own, other, own_grad, other_grad, depth, block=1792):
    tokens, columns = own_grad.shape
    x_spec = pl.BlockSpec((HALF, block), lambda k: (0, k))
    grad_spec = pl.BlockSpec(own_grad.shape, lambda k: (0, 0))
    return pl.pallas_call(
        head_grad_kernel,
        out_shape=jax.ShapeDtypeStruct((depth, columns), own_grad.dtype),
        grid=(depth // block,),
        in_specs=[x_spec, x_spec, grad_spec, grad_spec],
        out_specs=pl.BlockSpec((block, columns), lambda k: (k, 0)),
        compiler_params=pltpu.CompilerParams(vmem_limit_bytes=16 * MIB),
        cost_estimate=pl.CostEstimate(
            flops=4 * tokens * depth * columns, bytes_accessed=2 * depth * (columns + 2 * tokens), transcendentals=0
        ),
        name="head_grad",
    )(own, other, own_grad, other_grad)


def local(hidden, head_weight, ref_logprobs, token_ids, response_mask, advantages):
    depth, columns = head_weight.shape
    other_weight = pltpu.with_memory_space_constraint(swap_cores(head_weight), pltpu.VMEM)
    weight = pltpu.with_memory_space_constraint(head_weight, pltpu.VMEM)

    sent = pack(hidden, ref_logprobs, columns)
    sent = spread(exchange(sent, FIRST), depth, columns)
    own = exchange(sent, SECOND).reshape(HALF, depth + 2 * columns)
    other = swap_cores(own)

    tokens = (token_ids, response_mask, advantages)
    near = pltpu.with_memory_space_constraint(own, pltpu.VMEM)
    logits, stats, token = local_logits(near, weight, other_weight, tokens, 64)
    stats = lax.all_to_all(stats, CHIPS, split_axis=0, concat_axis=0, tiled=True)

    grad, theirs, part = hidden_grad(logits, near, stats, token, weight, other_weight)
    grad_head = head_grad(own, other, grad, swap_cores(theirs), depth)

    part = exchange(part.reshape(PEERS, PEERS * ROWS, depth), SECOND)
    part = add_up(part)
    part, grad_head = lax.optimization_barrier((part.reshape(PEERS, ROWS, depth), grad_head))
    grad_hidden = add_up(exchange(part, FIRST))
    return grad_hidden, grad_head


def solution(mesh):
    fine = Mesh(mesh.devices.reshape(SIZES), AXES)
    return jax.shard_map(
        local,
        mesh=fine,
        in_specs=(P(AXES, None), P(None, AXES), P(AXES, None), P(), P(), P()),
        out_specs=(P(AXES, None), P(None, AXES)),
        check_vma=False,
    )
```

```python
import functools

import jax
import jax.numpy as jnp
import numpy as np
from jax import lax
from jax.experimental import pallas as pl
from jax.experimental.pallas import tpu as pltpu
from jax.sharding import Mesh
from jax.sharding import PartitionSpec as P

grad_scale = 256.0

AXES = ("yh", "core", "x", "yl", "z")
CHIPS = ("yh", "x", "yl", "z")
SIZES = (2, 2, 4, 2, 4)
PEERS = 8
ROWS = 2
HALF = 128
MIB = 1 << 20


def device_at(x, y, z, core):
    return int(np.ravel_multi_index((y // 2, core, x, y % 2, z), SIZES))


PLACE = {(0, 0): 0, (1, 0): 1, (1, 1): 2, (0, 1): 3}


def chip(e, f):
    return tuple(PLACE[(e >> k) & 1, (f >> k) & 1] for k in (2, 1, 0))


def device(core, first, second, to=None):
    place = chip(first, second) if core == 0 else chip(second, first)
    return device_at(*place, core if to is None else to)


FIRST = [[device(c, v, s) for v in range(8)] for c in (0, 1) for s in range(8)]
SECOND = [[device(c, s, v) for v in range(8)] for c in (0, 1) for s in range(8)]
ORDER = [
    [ROWS * device(c, first, second) + r for second in range(8) for first in range(8) for r in range(ROWS)]
    for c in (0, 1)
]

def exchange(x, groups):
    return lax.all_to_all(
        x, AXES, split_axis=0, concat_axis=0, axis_index_groups=groups, tiled=True
    )


def swap_cores(x):
    return lax.ppermute(x, "core", [(0, 1), (1, 0)])


def pack_kernel(columns, hidden_ref, ref_ref, out_ref):
    core = lax.axis_index("core")
    for mine in (0, 1):

        @pl.when(core == mine)
        def _(mine=mine):
            for first in range(PEERS):
                target = 0
                for second in range(PEERS):
                    for to in (mine, 1 - mine):
                        source = device(mine, first, second, to) * columns
                        out_ref[first, :, target : target + columns] = ref_ref[:, source : source + columns]
                        target += columns

    rows = hidden_ref[...]
    for peer in range(PEERS):
        out_ref[peer, :, 2 * PEERS * columns :] = rows


def pack(hidden, ref_logprobs, columns):
    width = 2 * PEERS * columns + hidden.shape[1]
    whole = lambda shape: pl.BlockSpec(shape, lambda i: (0,) * len(shape))
    return pl.pallas_call(
        functools.partial(pack_kernel, columns),
        out_shape=jax.ShapeDtypeStruct((PEERS, ROWS, width), hidden.dtype),
        grid=(1,),
        in_specs=[whole(hidden.shape), whole(ref_logprobs.shape)],
        out_specs=whole((PEERS, ROWS, width)),
        compiler_params=pltpu.CompilerParams(vmem_limit_bytes=8 * MIB),
        name="pack",
    )(pltpu.with_memory_space_constraint(hidden, pltpu.HBM), pltpu.with_memory_space_constraint(ref_logprobs, pltpu.HBM))


def spread_kernel(columns, in_ref, rows_ref, lp_ref):
    depth = rows_ref.shape[1]
    first = in_ref.shape[2] - depth

    def rows(start, size):
        parts = [in_ref[peer, :, start : start + size].astype(jnp.float32) for peer in range(PEERS)]
        return jnp.concatenate(parts, axis=0).astype(rows_ref.dtype)

    block = 512
    for start in range(0, depth, block):
        rows_ref[:, start : start + block] = rows(first + start, block)
    for peer in range(PEERS):
        lp_ref[peer] = rows(peer * 2 * columns, 2 * columns)


def spread(got, depth, columns):
    vmem = pl.BlockSpec(memory_space=pltpu.VMEM)
    rows, lp = pl.pallas_call(
        functools.partial(spread_kernel, columns),
        out_shape=(
            jax.ShapeDtypeStruct((PEERS * ROWS, depth), got.dtype),
            jax.ShapeDtypeStruct((PEERS, PEERS * ROWS, 2 * columns), got.dtype),
        ),
        in_specs=[vmem],
        out_specs=(vmem, vmem),
        compiler_params=pltpu.CompilerParams(vmem_limit_bytes=8 * MIB),
        name="spread",
    )(got)
    rows = jnp.broadcast_to(rows[None], (PEERS,) + rows.shape)
    return jnp.concatenate([rows, lp], axis=2)


def token_order(core):
    place = lax.broadcasted_iota(jnp.int32, (1, HALF), 1)
    second, first, row = place >> 4, (place >> 1) & 7, place & 1
    e = jnp.where(core == 0, first, second)
    f = first + second - e
    low = e ^ f
    bit = lambda v, k: (v >> k) & 1
    index = bit(f, 1) * 2 + core
    index = index * 4 + 2 * bit(f, 2) + bit(low, 2)
    index = index * 2 + bit(low, 1)
    index = index * 4 + 2 * bit(f, 0) + bit(low, 0)
    return ROWS * index + row


def token_lines(columns, id_ref, mask_ref, advantage_ref):
    core = lax.axis_index("core")
    mine = lax.axis_index(AXES)
    other = mine + (1 - 2 * core) * (SIZES[2] * SIZES[3] * SIZES[4])
    tokens = id_ref.shape[1]
    lines = [
        id_ref[...].astype(jnp.float32),
        grad_scale * mask_ref[...].astype(jnp.float32),
        advantage_ref[...],
        jnp.zeros((HALF - 3, tokens), jnp.float32),
    ]
    table = jnp.concatenate(lines, axis=0).T
    here = lax.broadcasted_iota(jnp.int32, (tokens, HALF), 0) == token_order(core)
    ids, weighting, advantage = (
        jnp.sum(jnp.where(here, table[:, i : i + 1], 0.0), axis=0, keepdims=True) for i in range(3)
    )
    places = [ids - (d * columns).astype(jnp.float32) for d in (mine, other)]
    return jnp.concatenate(places + [weighting, advantage, jnp.zeros((4, HALF), jnp.float32)], axis=0)


def logits_kernel(
    block, own_ref, weight_ref, other_weight_ref, id_ref, mask_ref, advantage_ref, logits_ref, stats_ref, token_ref
):
    depth, columns = weight_ref.shape
    for side, w_ref in enumerate((weight_ref, other_weight_ref)):
        here = slice(side * columns, (side + 1) * columns)
        for step in range(depth // block):
            rows = slice(step * block, (step + 1) * block)
            part = jnp.dot(own_ref[:, rows], w_ref[rows, :], preferred_element_type=jnp.float32)
            if step == 0:
                logits_ref[:, here] = part
            else:
                logits_ref[:, here] += part
    token_ref[...] = token_lines(columns, id_ref, mask_ref, advantage_ref)
    logits = logits_ref[...]
    top = jnp.max(logits, axis=1, keepdims=True)
    shifted = logits - top
    scaled = jnp.exp(shifted)
    total = jnp.sum(scaled, axis=1, keepdims=True)
    cross = jnp.sum(scaled * (shifted - own_ref[:, depth:].astype(jnp.float32)), axis=1, keepdims=True)
    lane = lax.broadcasted_iota(jnp.int32, (HALF, HALF), 1)
    tile = jnp.where(lane == 0, top, jnp.where(lane == 1, total, cross)).T[:8]
    stats_ref[...] = jnp.broadcast_to(tile[None], stats_ref.shape)


def local_logits(own, weight, other_weight, tokens, peers, block=1024):
    depth, columns = weight.shape
    vmem = pl.BlockSpec(memory_space=pltpu.VMEM)
    return pl.pallas_call(
        functools.partial(logits_kernel, block),
        out_shape=(
            jax.ShapeDtypeStruct((HALF, 2 * columns), jnp.float32),
            jax.ShapeDtypeStruct((peers, 8, HALF), jnp.float32),
            jax.ShapeDtypeStruct((8, HALF), jnp.float32),
        ),
        in_specs=[vmem] * 6,
        out_specs=(vmem,) * 3,
        compiler_params=pltpu.CompilerParams(vmem_limit_bytes=16 * MIB),
        cost_estimate=pl.CostEstimate(
            flops=4 * HALF * depth * columns, bytes_accessed=4 * depth * columns, transcendentals=0
        ),
        name="logits",
    )(own, weight, other_weight, *(v.reshape(1, -1) for v in tokens))


def hidden_grad_kernel(
    block, logits_ref, own_ref, stats_ref, token_ref, weight_ref, other_weight_ref,
    near_ref, far_ref, out_ref, grad_ref, other_grad_ref, sums, sems,
):
    depth, columns = weight_ref.shape
    steps = depth // block
    tops, totals, crosses = (stats_ref[:, i, :] for i in range(3))
    top = jnp.max(tops, axis=0, keepdims=True)
    below = tops - top
    factor = jnp.exp(below)
    total = jnp.sum(factor * totals, axis=0, keepdims=True)
    cross = jnp.sum(factor * (crosses + below * totals), axis=0, keepdims=True)
    log_total = jnp.log(total)
    divergence = cross / total - log_total
    lines = [top, log_total, divergence, token_ref[0:4, :], jnp.zeros((HALF - 7, HALF), jnp.float32)]
    table = jnp.concatenate(lines, axis=0).T
    row_top, row_log, row_div, place, other_place, weighting, advantage = (table[:, i : i + 1] for i in range(7))
    for side, (g_ref, chosen) in enumerate(((grad_ref, place), (other_grad_ref, other_place))):
        here = slice(side * columns, (side + 1) * columns)
        log_probs = (logits_ref[:, here] - row_top) - row_log
        chance = jnp.exp(log_probs)
        entry = lax.broadcasted_iota(jnp.int32, log_probs.shape, 1).astype(jnp.float32)
        picked = jnp.where(entry == chosen, 1.0, 0.0)
        lp = own_ref[:, depth + side * columns : depth + (side + 1) * columns].astype(jnp.float32)
        grad = weighting * (chance * (log_probs - lp - row_div) - advantage * (picked - chance))
        g_ref[...] = grad.astype(g_ref.dtype)

    def copy(step):
        if step >= steps:
            pair = ((grad_ref, near_ref), (other_grad_ref, far_ref))[step - steps]
            return pltpu.make_async_copy(*pair, sems.at[step])
        here = pl.ds(step * block, block)
        return pltpu.make_async_copy(sums.at[:, here], out_ref.at[:, here], sems.at[step])

    copy(steps).start()
    copy(steps + 1).start()

    for step in range(depth // block):
        here = slice(step * block, (step + 1) * block)
        total = [
            lax.dot_general(w_ref[here, :], g_ref[...], (((1,), (1,)), ((), ())), preferred_element_type=jnp.float32)
            for g_ref, w_ref in ((grad_ref, weight_ref), (other_grad_ref, other_weight_ref))
        ]
        sums[:, here] = (total[0] + total[1]).T.astype(sums.dtype)
        copy(step).start()
    for step in range(steps + 2):
        copy(step).wait()


def hidden_grad(logits, own, stats, token, weight, other_weight, block=1024):
    depth, columns = weight.shape
    part = pltpu.HBM((HALF, columns), weight.dtype)
    return pl.pallas_call(
        functools.partial(hidden_grad_kernel, block),
        out_shape=(part, part, pltpu.HBM((HALF, depth), weight.dtype)),
        in_specs=[pl.BlockSpec(memory_space=pltpu.VMEM)] * 6,
        out_specs=(pl.BlockSpec(memory_space=pltpu.HBM),) * 3,
        scratch_shapes=[
            pltpu.VMEM((HALF, columns), weight.dtype),
            pltpu.VMEM((HALF, columns), weight.dtype),
            pltpu.VMEM((HALF, depth), weight.dtype),
            pltpu.SemaphoreType.DMA((depth // block + 2,)),
        ],
        compiler_params=pltpu.CompilerParams(vmem_limit_bytes=16 * MIB),
        cost_estimate=pl.CostEstimate(
            flops=8 * HALF * depth * columns, bytes_accessed=4 * depth * columns, transcendentals=0
        ),
        name="hidden_grad",
    )(logits, own, stats, token, weight, other_weight)


def total_of(parts):
    parts = [p.astype(jnp.float32) for p in parts]
    while len(parts) > 1:
        parts = [a + b for a, b in zip(parts[::2], parts[1::2])]
    return parts[0]


def sum_far_kernel(block, part_ref, out_ref, here_ref, sems):
    steps = part_ref.shape[2] // block

    def load(step):
        columns = pl.ds(step * block, block)
        return pltpu.make_async_copy(part_ref.at[:, :, columns], here_ref.at[:, :, columns], sems.at[step])

    for step in range(steps):
        load(step).start()
    for step in range(steps):
        load(step).wait()
        columns = slice(step * block, (step + 1) * block)
        total = total_of([here_ref[peer, :, columns] for peer in range(PEERS)])
        out_ref[:, columns] = total.astype(out_ref.dtype)


def sum_kernel(part_ref, out_ref):
    out_ref[...] = total_of([part_ref[peer] for peer in range(PEERS)]).astype(out_ref.dtype)


def add_up(parts, block=None):
    vmem = pl.BlockSpec(memory_space=pltpu.VMEM)
    space = pltpu.HBM if block else pltpu.VMEM
    return pl.pallas_call(
        functools.partial(sum_far_kernel, block) if block else sum_kernel,
        out_shape=jax.ShapeDtypeStruct(parts.shape[1:], parts.dtype),
        in_specs=[pl.BlockSpec(memory_space=space)],
        out_specs=vmem,
        scratch_shapes=(
            [pltpu.VMEM(parts.shape, parts.dtype), pltpu.SemaphoreType.DMA((parts.shape[2] // block,))] if block else []
        ),
        compiler_params=pltpu.CompilerParams(vmem_limit_bytes=8 * MIB),
        name="add_up",
    )(pltpu.with_memory_space_constraint(parts, space))


def head_grad_kernel(own_ref, other_ref, own_grad_ref, other_grad_ref, out_ref):
    x = jnp.concatenate([own_ref[...], other_ref[...]], axis=0)
    grad = jnp.concatenate([own_grad_ref[...], other_grad_ref[...]], axis=0)
    out_ref[...] = lax.dot_general(
        x, grad, (((0,), (0,)), ((), ())), preferred_element_type=jnp.float32
    ).astype(out_ref.dtype)


def head_grad(own, other, own_grad, other_grad, depth, block=1792):
    tokens, columns = own_grad.shape
    x_spec = pl.BlockSpec((HALF, block), lambda k: (0, k))
    grad_spec = pl.BlockSpec(own_grad.shape, lambda k: (0, 0))
    return pl.pallas_call(
        head_grad_kernel,
        out_shape=jax.ShapeDtypeStruct((depth, columns), own_grad.dtype),
        grid=(depth // block,),
        in_specs=[x_spec, x_spec, grad_spec, grad_spec],
        out_specs=pl.BlockSpec((block, columns), lambda k: (k, 0)),
        compiler_params=pltpu.CompilerParams(vmem_limit_bytes=16 * MIB),
        cost_estimate=pl.CostEstimate(
            flops=4 * tokens * depth * columns, bytes_accessed=2 * depth * (columns + 2 * tokens), transcendentals=0
        ),
        name="head_grad",
    )(*(pltpu.with_memory_space_constraint(x, pltpu.HBM) for x in (own, other)), own_grad, other_grad)


def local(hidden, head_weight, ref_logprobs, token_ids, response_mask, advantages):
    depth, columns = head_weight.shape
    other_weight = pltpu.with_memory_space_constraint(swap_cores(head_weight), pltpu.VMEM)
    weight = pltpu.with_memory_space_constraint(head_weight, pltpu.VMEM)

    sent = pack(hidden, ref_logprobs, columns)
    sent = spread(exchange(sent, FIRST), depth, columns)
    own = exchange(sent, SECOND).reshape(HALF, depth + 2 * columns)

    tokens = (token_ids, response_mask, advantages)
    near = pltpu.with_memory_space_constraint(own, pltpu.VMEM)
    logits, stats, token = local_logits(near, weight, other_weight, tokens, 64)
    stats = lax.all_to_all(stats, CHIPS, split_axis=0, concat_axis=0, tiled=True)
    late, stats = lax.optimization_barrier((own, stats))
    other = swap_cores(late)

    grad, theirs, part = hidden_grad(logits, near, stats, token, weight, other_weight)
    grad_head = head_grad(own, other, grad, swap_cores(theirs), depth)

    part = exchange(part.reshape(PEERS, PEERS * ROWS, depth), SECOND)
    part, grad_head = lax.optimization_barrier((part, grad_head))
    part = add_up(part, 1792)
    grad_hidden = add_up(exchange(part.reshape(PEERS, ROWS, depth), FIRST))
    return grad_hidden, grad_head


def solution(mesh):
    fine = Mesh(mesh.devices.reshape(SIZES), AXES)
    return jax.shard_map(
        local,
        mesh=fine,
        in_specs=(P(AXES, None), P(None, AXES), P(AXES, None), P(), P(), P()),
        out_specs=(P(AXES, None), P(None, AXES)),
        check_vma=False,
    )
```

```python
import functools

import jax
import jax.numpy as jnp
import numpy as np
from jax import lax
from jax.experimental import pallas as pl
from jax.experimental.pallas import tpu as pltpu
from jax.sharding import Mesh
from jax.sharding import PartitionSpec as P

grad_scale = 256.0

AXES = ("yh", "core", "x", "yl", "z")
CHIPS = ("yh", "x", "yl", "z")
SIZES = (2, 2, 4, 2, 4)
PEERS = 8
ROWS = 2
HALF = 128
MIB = 1 << 20


def device_at(x, y, z, core):
    return int(np.ravel_multi_index((y // 2, core, x, y % 2, z), SIZES))


PLACE = {(0, 0): 0, (1, 0): 1, (1, 1): 2, (0, 1): 3}


def chip(e, f):
    return tuple(PLACE[(e >> k) & 1, (f >> k) & 1] for k in (2, 1, 0))


def device(core, first, second, to=None):
    place = chip(first, second) if core == 0 else chip(second, first)
    return device_at(*place, core if to is None else to)


FIRST = [[device(c, v, s) for v in range(8)] for c in (0, 1) for s in range(8)]
SECOND = [[device(c, s, v) for v in range(8)] for c in (0, 1) for s in range(8)]
ORDER = [
    [ROWS * device(c, first, second) + r for second in range(8) for first in range(8) for r in range(ROWS)]
    for c in (0, 1)
]

def exchange(x, groups):
    return lax.all_to_all(
        x, AXES, split_axis=0, concat_axis=0, axis_index_groups=groups, tiled=True
    )


def swap_cores(x):
    return lax.ppermute(x, "core", [(0, 1), (1, 0)])


def pack_kernel(columns, hidden_ref, ref_ref, out_ref):
    core = lax.axis_index("core")
    for mine in (0, 1):

        @pl.when(core == mine)
        def _(mine=mine):
            for first in range(PEERS):
                target = 0
                for second in range(PEERS):
                    for to in (mine, 1 - mine):
                        source = device(mine, first, second, to) * columns
                        out_ref[first, :, target : target + columns] = ref_ref[:, source : source + columns]
                        target += columns

    rows = hidden_ref[...]
    for peer in range(PEERS):
        out_ref[peer, :, 2 * PEERS * columns :] = rows


def pack(hidden, ref_logprobs, columns):
    width = 2 * PEERS * columns + hidden.shape[1]
    whole = lambda shape: pl.BlockSpec(shape, lambda i: (0,) * len(shape))
    return pl.pallas_call(
        functools.partial(pack_kernel, columns),
        out_shape=jax.ShapeDtypeStruct((PEERS, ROWS, width), hidden.dtype),
        grid=(1,),
        in_specs=[whole(hidden.shape), whole(ref_logprobs.shape)],
        out_specs=whole((PEERS, ROWS, width)),
        compiler_params=pltpu.CompilerParams(vmem_limit_bytes=8 * MIB),
        name="pack",
    )(pltpu.with_memory_space_constraint(hidden, pltpu.HBM), pltpu.with_memory_space_constraint(ref_logprobs, pltpu.HBM))


def spread_kernel(columns, in_ref, rows_ref, lp_ref):
    depth = rows_ref.shape[1]
    first = in_ref.shape[2] - depth

    def rows(start, size):
        parts = [in_ref[peer, :, start : start + size].astype(jnp.float32) for peer in range(PEERS)]
        return jnp.concatenate(parts, axis=0).astype(rows_ref.dtype)

    block = 512
    for start in range(0, depth, block):
        rows_ref[:, start : start + block] = rows(first + start, block)
    for peer in range(PEERS):
        lp_ref[peer] = rows(peer * 2 * columns, 2 * columns)


def spread(got, depth, columns):
    vmem = pl.BlockSpec(memory_space=pltpu.VMEM)
    rows, lp = pl.pallas_call(
        functools.partial(spread_kernel, columns),
        out_shape=(
            jax.ShapeDtypeStruct((PEERS * ROWS, depth), got.dtype),
            jax.ShapeDtypeStruct((PEERS, PEERS * ROWS, 2 * columns), got.dtype),
        ),
        in_specs=[vmem],
        out_specs=(vmem, vmem),
        compiler_params=pltpu.CompilerParams(vmem_limit_bytes=8 * MIB),
        name="spread",
    )(got)
    rows = jnp.broadcast_to(rows[None], (PEERS,) + rows.shape)
    return jnp.concatenate([rows, lp], axis=2)


def token_order(core):
    place = lax.broadcasted_iota(jnp.int32, (1, HALF), 1)
    second, first, row = place >> 4, (place >> 1) & 7, place & 1
    e = jnp.where(core == 0, first, second)
    f = first + second - e
    low = e ^ f
    bit = lambda v, k: (v >> k) & 1
    index = bit(f, 1) * 2 + core
    index = index * 4 + 2 * bit(f, 2) + bit(low, 2)
    index = index * 2 + bit(low, 1)
    index = index * 4 + 2 * bit(f, 0) + bit(low, 0)
    return ROWS * index + row


def token_lines(columns, id_ref, mask_ref, advantage_ref):
    core = lax.axis_index("core")
    mine = lax.axis_index(AXES)
    other = mine + (1 - 2 * core) * (SIZES[2] * SIZES[3] * SIZES[4])
    tokens = id_ref.shape[1]
    lines = [
        id_ref[...].astype(jnp.float32),
        grad_scale * mask_ref[...].astype(jnp.float32),
        advantage_ref[...],
        jnp.zeros((HALF - 3, tokens), jnp.float32),
    ]
    table = jnp.concatenate(lines, axis=0).T
    here = lax.broadcasted_iota(jnp.int32, (tokens, HALF), 0) == token_order(core)
    ids, weighting, advantage = (
        jnp.sum(jnp.where(here, table[:, i : i + 1], 0.0), axis=0, keepdims=True) for i in range(3)
    )
    places = [ids - (d * columns).astype(jnp.float32) for d in (mine, other)]
    return jnp.concatenate(places + [weighting, advantage, jnp.zeros((4, HALF), jnp.float32)], axis=0)


def logits_kernel(
    block, own_ref, weight_ref, other_weight_ref, id_ref, mask_ref, advantage_ref,
    logits_ref, stats_ref, token_ref, rows_ref, sem,
):
    depth, columns = weight_ref.shape
    leave = pltpu.make_async_copy(own_ref.at[:, pl.ds(0, depth)], rows_ref, sem)
    leave.start()
    for side, w_ref in enumerate((weight_ref, other_weight_ref)):
        here = slice(side * columns, (side + 1) * columns)
        for step in range(depth // block):
            rows = slice(step * block, (step + 1) * block)
            part = jnp.dot(own_ref[:, rows], w_ref[rows, :], preferred_element_type=jnp.float32)
            if step == 0:
                logits_ref[:, here] = part
            else:
                logits_ref[:, here] += part
    token_ref[...] = token_lines(columns, id_ref, mask_ref, advantage_ref)
    logits = logits_ref[...]
    top = jnp.max(logits, axis=1, keepdims=True)
    shifted = logits - top
    scaled = jnp.exp(shifted)
    total = jnp.sum(scaled, axis=1, keepdims=True)
    cross = jnp.sum(scaled * (shifted - own_ref[:, depth:].astype(jnp.float32)), axis=1, keepdims=True)
    lane = lax.broadcasted_iota(jnp.int32, (HALF, HALF), 1)
    tile = jnp.where(lane == 0, top, jnp.where(lane == 1, total, cross)).T[:8]
    stats_ref[...] = jnp.broadcast_to(tile[None], stats_ref.shape)
    leave.wait()


def local_logits(own, weight, other_weight, tokens, peers, block=1024):
    depth, columns = weight.shape
    vmem = pl.BlockSpec(memory_space=pltpu.VMEM)
    return pl.pallas_call(
        functools.partial(logits_kernel, block),
        out_shape=(
            jax.ShapeDtypeStruct((HALF, 2 * columns), jnp.float32),
            jax.ShapeDtypeStruct((peers, 8, HALF), jnp.float32),
            jax.ShapeDtypeStruct((8, HALF), jnp.float32),
            pltpu.HBM((HALF, depth), own.dtype),
        ),
        in_specs=[vmem] * 6,
        out_specs=(vmem, vmem, vmem, pl.BlockSpec(memory_space=pltpu.HBM)),
        scratch_shapes=[pltpu.SemaphoreType.DMA],
        compiler_params=pltpu.CompilerParams(vmem_limit_bytes=16 * MIB),
        cost_estimate=pl.CostEstimate(
            flops=4 * HALF * depth * columns, bytes_accessed=4 * depth * columns, transcendentals=0
        ),
        name="logits",
    )(own, weight, other_weight, *(v.reshape(1, -1) for v in tokens))


def hidden_grad_kernel(
    block, logits_ref, own_ref, stats_ref, token_ref, weight_ref, other_weight_ref,
    near_ref, far_ref, out_ref, grad_ref, other_grad_ref, sums, sems,
):
    depth, columns = weight_ref.shape
    steps = depth // block
    tops, totals, crosses = (stats_ref[:, i, :] for i in range(3))
    top = jnp.max(tops, axis=0, keepdims=True)
    below = tops - top
    factor = jnp.exp(below)
    total = jnp.sum(factor * totals, axis=0, keepdims=True)
    cross = jnp.sum(factor * (crosses + below * totals), axis=0, keepdims=True)
    log_total = jnp.log(total)
    divergence = cross / total - log_total
    lines = [top, log_total, divergence, token_ref[0:4, :], jnp.zeros((HALF - 7, HALF), jnp.float32)]
    table = jnp.concatenate(lines, axis=0).T
    row_top, row_log, row_div, place, other_place, weighting, advantage = (table[:, i : i + 1] for i in range(7))
    for side, (g_ref, chosen) in enumerate(((grad_ref, place), (other_grad_ref, other_place))):
        here = slice(side * columns, (side + 1) * columns)
        log_probs = (logits_ref[:, here] - row_top) - row_log
        chance = jnp.exp(log_probs)
        entry = lax.broadcasted_iota(jnp.int32, log_probs.shape, 1).astype(jnp.float32)
        picked = jnp.where(entry == chosen, 1.0, 0.0)
        lp = own_ref[:, depth + side * columns : depth + (side + 1) * columns].astype(jnp.float32)
        grad = weighting * (chance * (log_probs - lp - row_div) - advantage * (picked - chance))
        g_ref[...] = grad.astype(g_ref.dtype)

    def copy(step):
        if step >= steps:
            pair = ((grad_ref, near_ref), (other_grad_ref, far_ref))[step - steps]
            return pltpu.make_async_copy(*pair, sems.at[step])
        here = pl.ds(step * block, block)
        return pltpu.make_async_copy(sums.at[:, here], out_ref.at[:, here], sems.at[step])

    copy(steps).start()
    copy(steps + 1).start()

    for step in range(depth // block):
        here = slice(step * block, (step + 1) * block)
        total = [
            lax.dot_general(w_ref[here, :], g_ref[...], (((1,), (1,)), ((), ())), preferred_element_type=jnp.float32)
            for g_ref, w_ref in ((grad_ref, weight_ref), (other_grad_ref, other_weight_ref))
        ]
        sums[:, here] = (total[0] + total[1]).T.astype(sums.dtype)
        copy(step).start()
    for step in range(steps + 2):
        copy(step).wait()


def hidden_grad(logits, own, stats, token, weight, other_weight, block=1024):
    depth, columns = weight.shape
    part = pltpu.HBM((HALF, columns), weight.dtype)
    return pl.pallas_call(
        functools.partial(hidden_grad_kernel, block),
        out_shape=(part, part, pltpu.HBM((HALF, depth), weight.dtype)),
        in_specs=[pl.BlockSpec(memory_space=pltpu.VMEM)] * 6,
        out_specs=(pl.BlockSpec(memory_space=pltpu.HBM),) * 3,
        scratch_shapes=[
            pltpu.VMEM((HALF, columns), weight.dtype),
            pltpu.VMEM((HALF, columns), weight.dtype),
            pltpu.VMEM((HALF, depth), weight.dtype),
            pltpu.SemaphoreType.DMA((depth // block + 2,)),
        ],
        compiler_params=pltpu.CompilerParams(vmem_limit_bytes=16 * MIB),
        cost_estimate=pl.CostEstimate(
            flops=8 * HALF * depth * columns, bytes_accessed=4 * depth * columns, transcendentals=0
        ),
        name="hidden_grad",
    )(logits, own, stats, token, weight, other_weight)


def total_of(parts):
    parts = [p.astype(jnp.float32) for p in parts]
    while len(parts) > 1:
        parts = [a + b for a, b in zip(parts[::2], parts[1::2])]
    return parts[0]


def sum_kernel(part_ref, out_ref):
    out_ref[...] = total_of([part_ref[peer] for peer in range(PEERS)]).astype(out_ref.dtype)


def add_up(parts):
    vmem = pl.BlockSpec(memory_space=pltpu.VMEM)
    return pl.pallas_call(
        sum_kernel,
        out_shape=jax.ShapeDtypeStruct(parts.shape[1:], parts.dtype),
        in_specs=[vmem],
        out_specs=vmem,
        compiler_params=pltpu.CompilerParams(vmem_limit_bytes=8 * MIB),
        name="add_up",
    )(pltpu.with_memory_space_constraint(parts, pltpu.VMEM))


def head_grad_kernel(own_ref, other_ref, own_grad_ref, other_grad_ref, out_ref):
    x = jnp.concatenate([own_ref[...], other_ref[...]], axis=0)
    grad = jnp.concatenate([own_grad_ref[...], other_grad_ref[...]], axis=0)
    out_ref[...] = lax.dot_general(
        x, grad, (((0,), (0,)), ((), ())), preferred_element_type=jnp.float32
    ).astype(out_ref.dtype)


def head_grad(own, other, own_grad, other_grad, depth, block=1792):
    tokens, columns = own_grad.shape
    x_spec = pl.BlockSpec((HALF, block), lambda k: (0, k))
    grad_spec = pl.BlockSpec(own_grad.shape, lambda k: (0, 0))
    return pl.pallas_call(
        head_grad_kernel,
        out_shape=jax.ShapeDtypeStruct((depth, columns), own_grad.dtype),
        grid=(depth // block,),
        in_specs=[x_spec, x_spec, grad_spec, grad_spec],
        out_specs=pl.BlockSpec((block, columns), lambda k: (k, 0)),
        compiler_params=pltpu.CompilerParams(vmem_limit_bytes=16 * MIB),
        cost_estimate=pl.CostEstimate(
            flops=4 * tokens * depth * columns, bytes_accessed=2 * depth * (columns + 2 * tokens), transcendentals=0
        ),
        name="head_grad",
    )(*(pltpu.with_memory_space_constraint(x, pltpu.HBM) for x in (own, other)), own_grad, other_grad)


def local(hidden, head_weight, ref_logprobs, token_ids, response_mask, advantages):
    depth, columns = head_weight.shape
    other_weight = pltpu.with_memory_space_constraint(swap_cores(head_weight), pltpu.VMEM)
    weight = pltpu.with_memory_space_constraint(head_weight, pltpu.VMEM)

    sent = pack(hidden, ref_logprobs, columns)
    sent = spread(exchange(sent, FIRST), depth, columns)
    own = exchange(sent, SECOND).reshape(HALF, depth + 2 * columns)

    tokens = (token_ids, response_mask, advantages)
    near = pltpu.with_memory_space_constraint(own, pltpu.VMEM)
    logits, stats, token, rows = local_logits(near, weight, other_weight, tokens, 64)
    stats = lax.all_to_all(stats, CHIPS, split_axis=0, concat_axis=0, tiled=True)
    rows, stats = lax.optimization_barrier((rows, stats))
    other = swap_cores(rows)

    grad, theirs, part = hidden_grad(logits, near, stats, token, weight, other_weight)
    grad_head = head_grad(rows, other, grad, swap_cores(theirs), depth)

    part = exchange(part.reshape(PEERS, PEERS * ROWS, depth), SECOND)
    part, grad_head = lax.optimization_barrier((part, grad_head))
    part = add_up(part)
    grad_hidden = add_up(exchange(part.reshape(PEERS, ROWS, depth), FIRST))
    return grad_hidden, grad_head


def solution(mesh):
    fine = Mesh(mesh.devices.reshape(SIZES), AXES)
    return jax.shard_map(
        local,
        mesh=fine,
        in_specs=(P(AXES, None), P(None, AXES), P(AXES, None), P(), P(), P()),
        out_specs=(P(AXES, None), P(None, AXES)),
        check_vma=False,
    )
```

```python
import functools

import jax
import jax.numpy as jnp
import numpy as np
from jax import lax
from jax.experimental import pallas as pl
from jax.experimental.pallas import tpu as pltpu
from jax.sharding import Mesh
from jax.sharding import PartitionSpec as P

grad_scale = 256.0

AXES = ("yh", "core", "x", "yl", "z")
CHIPS = ("yh", "x", "yl", "z")
SIZES = (2, 2, 4, 2, 4)
PEERS = 8
ROWS = 2
HALF = 128
MIB = 1 << 20


def device_at(x, y, z, core):
    return int(np.ravel_multi_index((y // 2, core, x, y % 2, z), SIZES))


PLACE = {(0, 0): 0, (1, 0): 1, (1, 1): 2, (0, 1): 3}


def chip(e, f):
    return tuple(PLACE[(e >> k) & 1, (f >> k) & 1] for k in (2, 1, 0))


def device(core, first, second, to=None):
    place = chip(first, second) if core == 0 else chip(second, first)
    return device_at(*place, core if to is None else to)


FIRST = [[device(c, v, s) for v in range(8)] for c in (0, 1) for s in range(8)]
SECOND = [[device(c, s, v) for v in range(8)] for c in (0, 1) for s in range(8)]
ORDER = [
    [ROWS * device(c, first, second) + r for second in range(8) for first in range(8) for r in range(ROWS)]
    for c in (0, 1)
]

def exchange(x, groups):
    return lax.all_to_all(
        x, AXES, split_axis=0, concat_axis=0, axis_index_groups=groups, tiled=True
    )


def swap_cores(x):
    return lax.ppermute(x, "core", [(0, 1), (1, 0)])


def pack_kernel(columns, hidden_ref, ref_ref, out_ref):
    core = lax.axis_index("core")
    for mine in (0, 1):

        @pl.when(core == mine)
        def _(mine=mine):
            for first in range(PEERS):
                target = 0
                for second in range(PEERS):
                    for to in (mine, 1 - mine):
                        source = device(mine, first, second, to) * columns
                        out_ref[first, :, target : target + columns] = ref_ref[:, source : source + columns]
                        target += columns

    rows = hidden_ref[...]
    for peer in range(PEERS):
        out_ref[peer, :, 2 * PEERS * columns :] = rows


def pack(hidden, ref_logprobs, columns):
    width = 2 * PEERS * columns + hidden.shape[1]
    whole = lambda shape: pl.BlockSpec(shape, lambda i: (0,) * len(shape))
    return pl.pallas_call(
        functools.partial(pack_kernel, columns),
        out_shape=jax.ShapeDtypeStruct((PEERS, ROWS, width), hidden.dtype),
        grid=(1,),
        in_specs=[whole(hidden.shape), whole(ref_logprobs.shape)],
        out_specs=whole((PEERS, ROWS, width)),
        compiler_params=pltpu.CompilerParams(vmem_limit_bytes=8 * MIB),
        name="pack",
    )(pltpu.with_memory_space_constraint(hidden, pltpu.HBM), pltpu.with_memory_space_constraint(ref_logprobs, pltpu.HBM))


def spread_kernel(columns, in_ref, rows_ref, lp_ref):
    depth = rows_ref.shape[1]
    first = in_ref.shape[2] - depth

    def rows(start, size):
        parts = [in_ref[peer, :, start : start + size].astype(jnp.float32) for peer in range(PEERS)]
        return jnp.concatenate(parts, axis=0).astype(rows_ref.dtype)

    block = 512
    for start in range(0, depth, block):
        rows_ref[:, start : start + block] = rows(first + start, block)
    for peer in range(PEERS):
        lp_ref[peer] = rows(peer * 2 * columns, 2 * columns)


def spread(got, depth, columns):
    vmem = pl.BlockSpec(memory_space=pltpu.VMEM)
    rows, lp = pl.pallas_call(
        functools.partial(spread_kernel, columns),
        out_shape=(
            jax.ShapeDtypeStruct((PEERS * ROWS, depth), got.dtype),
            jax.ShapeDtypeStruct((PEERS, PEERS * ROWS, 2 * columns), got.dtype),
        ),
        in_specs=[vmem],
        out_specs=(vmem, vmem),
        compiler_params=pltpu.CompilerParams(vmem_limit_bytes=8 * MIB),
        name="spread",
    )(got)
    rows = jnp.broadcast_to(rows[None], (PEERS,) + rows.shape)
    return jnp.concatenate([rows, lp], axis=2)


def token_order(core):
    place = lax.broadcasted_iota(jnp.int32, (1, HALF), 1)
    second, first, row = place >> 4, (place >> 1) & 7, place & 1
    e = jnp.where(core == 0, first, second)
    f = first + second - e
    low = e ^ f
    bit = lambda v, k: (v >> k) & 1
    index = bit(f, 1) * 2 + core
    index = index * 4 + 2 * bit(f, 2) + bit(low, 2)
    index = index * 2 + bit(low, 1)
    index = index * 4 + 2 * bit(f, 0) + bit(low, 0)
    return ROWS * index + row


def token_lines(columns, id_ref, mask_ref, advantage_ref):
    core = lax.axis_index("core")
    mine = lax.axis_index(AXES)
    other = mine + (1 - 2 * core) * (SIZES[2] * SIZES[3] * SIZES[4])
    tokens = id_ref.shape[1]
    lines = [
        id_ref[...].astype(jnp.float32),
        grad_scale * mask_ref[...].astype(jnp.float32),
        advantage_ref[...],
        jnp.zeros((HALF - 3, tokens), jnp.float32),
    ]
    table = jnp.concatenate(lines, axis=0).T
    here = lax.broadcasted_iota(jnp.int32, (tokens, HALF), 0) == token_order(core)
    ids, weighting, advantage = (
        jnp.sum(jnp.where(here, table[:, i : i + 1], 0.0), axis=0, keepdims=True) for i in range(3)
    )
    places = [ids - (d * columns).astype(jnp.float32) for d in (mine, other)]
    return jnp.concatenate(places + [weighting, advantage, jnp.zeros((4, HALF), jnp.float32)], axis=0)


def logits_kernel(
    block, own_ref, weight_ref, other_weight_ref, id_ref, mask_ref, advantage_ref,
    logits_ref, stats_ref, token_ref, low_ref, high_ref, sems,
):
    depth, columns = weight_ref.shape
    half = HALF // 2
    leave = [
        pltpu.make_async_copy(own_ref.at[pl.ds(i * half, half), pl.ds(0, depth)], ref, sems.at[i])
        for i, ref in enumerate((low_ref, high_ref))
    ]
    for copy in leave:
        copy.start()
    for side, w_ref in enumerate((weight_ref, other_weight_ref)):
        here = slice(side * columns, (side + 1) * columns)
        for step in range(depth // block):
            rows = slice(step * block, (step + 1) * block)
            part = jnp.dot(own_ref[:, rows], w_ref[rows, :], preferred_element_type=jnp.float32)
            if step == 0:
                logits_ref[:, here] = part
            else:
                logits_ref[:, here] += part
    token_ref[...] = token_lines(columns, id_ref, mask_ref, advantage_ref)
    logits = logits_ref[...]
    top = jnp.max(logits, axis=1, keepdims=True)
    shifted = logits - top
    scaled = jnp.exp(shifted)
    total = jnp.sum(scaled, axis=1, keepdims=True)
    cross = jnp.sum(scaled * (shifted - own_ref[:, depth:].astype(jnp.float32)), axis=1, keepdims=True)
    lane = lax.broadcasted_iota(jnp.int32, (HALF, HALF), 1)
    tile = jnp.where(lane == 0, top, jnp.where(lane == 1, total, cross)).T[:8]
    stats_ref[...] = jnp.broadcast_to(tile[None], stats_ref.shape)
    for copy in leave:
        copy.wait()


def local_logits(own, weight, other_weight, tokens, peers, block=1024):
    depth, columns = weight.shape
    vmem = pl.BlockSpec(memory_space=pltpu.VMEM)
    return pl.pallas_call(
        functools.partial(logits_kernel, block),
        out_shape=(
            jax.ShapeDtypeStruct((HALF, 2 * columns), jnp.float32),
            jax.ShapeDtypeStruct((peers, 8, HALF), jnp.float32),
            jax.ShapeDtypeStruct((8, HALF), jnp.float32),
            pltpu.HBM((HALF // 2, depth), own.dtype),
            pltpu.HBM((HALF // 2, depth), own.dtype),
        ),
        in_specs=[vmem] * 6,
        out_specs=(vmem,) * 3 + (pl.BlockSpec(memory_space=pltpu.HBM),) * 2,
        scratch_shapes=[pltpu.SemaphoreType.DMA((2,))],
        compiler_params=pltpu.CompilerParams(vmem_limit_bytes=16 * MIB),
        cost_estimate=pl.CostEstimate(
            flops=4 * HALF * depth * columns, bytes_accessed=4 * depth * columns, transcendentals=0
        ),
        name="logits",
    )(own, weight, other_weight, *(v.reshape(1, -1) for v in tokens))


def hidden_grad_kernel(
    block, logits_ref, own_ref, stats_ref, token_ref, weight_ref, other_weight_ref,
    near_ref, far_ref, out_ref, grad_ref, other_grad_ref, sums, sems,
):
    depth, columns = weight_ref.shape
    steps = depth // block
    tops, totals, crosses = (stats_ref[:, i, :] for i in range(3))
    top = jnp.max(tops, axis=0, keepdims=True)
    below = tops - top
    factor = jnp.exp(below)
    total = jnp.sum(factor * totals, axis=0, keepdims=True)
    cross = jnp.sum(factor * (crosses + below * totals), axis=0, keepdims=True)
    log_total = jnp.log(total)
    divergence = cross / total - log_total
    lines = [top, log_total, divergence, token_ref[0:4, :], jnp.zeros((HALF - 7, HALF), jnp.float32)]
    table = jnp.concatenate(lines, axis=0).T
    row_top, row_log, row_div, place, other_place, weighting, advantage = (table[:, i : i + 1] for i in range(7))
    for side, (g_ref, chosen) in enumerate(((grad_ref, place), (other_grad_ref, other_place))):
        here = slice(side * columns, (side + 1) * columns)
        log_probs = (logits_ref[:, here] - row_top) - row_log
        chance = jnp.exp(log_probs)
        entry = lax.broadcasted_iota(jnp.int32, log_probs.shape, 1).astype(jnp.float32)
        picked = jnp.where(entry == chosen, 1.0, 0.0)
        lp = own_ref[:, depth + side * columns : depth + (side + 1) * columns].astype(jnp.float32)
        grad = weighting * (chance * (log_probs - lp - row_div) - advantage * (picked - chance))
        g_ref[...] = grad.astype(g_ref.dtype)

    def copy(step):
        if step >= steps:
            pair = ((grad_ref, near_ref), (other_grad_ref, far_ref))[step - steps]
            return pltpu.make_async_copy(*pair, sems.at[step])
        here = pl.ds(step * block, block)
        return pltpu.make_async_copy(sums.at[:, here], out_ref.at[:, here], sems.at[step])

    copy(steps).start()
    copy(steps + 1).start()

    for step in range(depth // block):
        here = slice(step * block, (step + 1) * block)
        total = [
            lax.dot_general(w_ref[here, :], g_ref[...], (((1,), (1,)), ((), ())), preferred_element_type=jnp.float32)
            for g_ref, w_ref in ((grad_ref, weight_ref), (other_grad_ref, other_weight_ref))
        ]
        sums[:, here] = (total[0] + total[1]).T.astype(sums.dtype)
        copy(step).start()
    for step in range(steps + 2):
        copy(step).wait()


def hidden_grad(logits, own, stats, token, weight, other_weight, block=1024):
    depth, columns = weight.shape
    part = pltpu.HBM((HALF, columns), weight.dtype)
    return pl.pallas_call(
        functools.partial(hidden_grad_kernel, block),
        out_shape=(part, part, pltpu.HBM((HALF, depth), weight.dtype)),
        in_specs=[pl.BlockSpec(memory_space=pltpu.VMEM)] * 6,
        out_specs=(pl.BlockSpec(memory_space=pltpu.HBM),) * 3,
        scratch_shapes=[
            pltpu.VMEM((HALF, columns), weight.dtype),
            pltpu.VMEM((HALF, columns), weight.dtype),
            pltpu.VMEM((HALF, depth), weight.dtype),
            pltpu.SemaphoreType.DMA((depth // block + 2,)),
        ],
        compiler_params=pltpu.CompilerParams(vmem_limit_bytes=16 * MIB),
        cost_estimate=pl.CostEstimate(
            flops=8 * HALF * depth * columns, bytes_accessed=4 * depth * columns, transcendentals=0
        ),
        name="hidden_grad",
    )(logits, own, stats, token, weight, other_weight)


def total_of(parts):
    parts = [p.astype(jnp.float32) for p in parts]
    while len(parts) > 1:
        parts = [a + b for a, b in zip(parts[::2], parts[1::2])]
    return parts[0]


def sum_kernel(part_ref, out_ref):
    out_ref[...] = total_of([part_ref[peer] for peer in range(PEERS)]).astype(out_ref.dtype)


def add_up(parts):
    vmem = pl.BlockSpec(memory_space=pltpu.VMEM)
    return pl.pallas_call(
        sum_kernel,
        out_shape=jax.ShapeDtypeStruct(parts.shape[1:], parts.dtype),
        in_specs=[vmem],
        out_specs=vmem,
        compiler_params=pltpu.CompilerParams(vmem_limit_bytes=8 * MIB),
        name="add_up",
    )(pltpu.with_memory_space_constraint(parts, pltpu.VMEM))


def head_grad_kernel(a_ref, b_ref, c_ref, d_ref, own_grad_ref, other_grad_ref, out_ref):
    x = jnp.concatenate([ref[...] for ref in (a_ref, b_ref, c_ref, d_ref)], axis=0)
    grad = jnp.concatenate([own_grad_ref[...], other_grad_ref[...]], axis=0)
    out_ref[...] = lax.dot_general(
        x, grad, (((0,), (0,)), ((), ())), preferred_element_type=jnp.float32
    ).astype(out_ref.dtype)


def head_grad(rows, own_grad, other_grad, depth, block=1792):
    tokens, columns = own_grad.shape
    x_spec = pl.BlockSpec((HALF // 2, block), lambda k: (0, k))
    grad_spec = pl.BlockSpec(own_grad.shape, lambda k: (0, 0))
    return pl.pallas_call(
        head_grad_kernel,
        out_shape=jax.ShapeDtypeStruct((depth, columns), own_grad.dtype),
        grid=(depth // block,),
        in_specs=[x_spec] * 4 + [grad_spec] * 2,
        out_specs=pl.BlockSpec((block, columns), lambda k: (k, 0)),
        compiler_params=pltpu.CompilerParams(vmem_limit_bytes=16 * MIB),
        cost_estimate=pl.CostEstimate(
            flops=4 * tokens * depth * columns, bytes_accessed=2 * depth * (columns + 2 * tokens), transcendentals=0
        ),
        name="head_grad",
    )(*(pltpu.with_memory_space_constraint(x, pltpu.HBM) for x in rows), own_grad, other_grad)


def local(hidden, head_weight, ref_logprobs, token_ids, response_mask, advantages):
    depth, columns = head_weight.shape
    other_weight = pltpu.with_memory_space_constraint(swap_cores(head_weight), pltpu.VMEM)
    weight = pltpu.with_memory_space_constraint(head_weight, pltpu.VMEM)

    sent = pack(hidden, ref_logprobs, columns)
    sent = spread(exchange(sent, FIRST), depth, columns)
    own = exchange(sent, SECOND).reshape(HALF, depth + 2 * columns)

    tokens = (token_ids, response_mask, advantages)
    near = pltpu.with_memory_space_constraint(own, pltpu.VMEM)
    logits, stats, token, *rows = local_logits(near, weight, other_weight, tokens, 64)
    stats = lax.all_to_all(stats, CHIPS, split_axis=0, concat_axis=0, tiled=True)

    grad, theirs, part = hidden_grad(logits, near, stats, token, weight, other_weight)
    *late, theirs = lax.optimization_barrier((*rows, theirs))
    grad_head = head_grad((*rows, *map(swap_cores, late)), grad, swap_cores(theirs), depth)

    part = exchange(part.reshape(PEERS, PEERS * ROWS, depth), SECOND)
    part, grad_head = lax.optimization_barrier((part, grad_head))
    part = add_up(part)
    grad_hidden = add_up(exchange(part.reshape(PEERS, ROWS, depth), FIRST))
    return grad_hidden, grad_head


def solution(mesh):
    fine = Mesh(mesh.devices.reshape(SIZES), AXES)
    return jax.shard_map(
        local,
        mesh=fine,
        in_specs=(P(AXES, None), P(None, AXES), P(AXES, None), P(), P(), P()),
        out_specs=(P(AXES, None), P(None, AXES)),
        check_vma=False,
    )
```

```python
import functools

import jax
import jax.numpy as jnp
import numpy as np
from jax import lax
from jax.experimental import pallas as pl
from jax.experimental.pallas import tpu as pltpu
from jax.sharding import Mesh
from jax.sharding import PartitionSpec as P

grad_scale = 256.0

AXES = ("yh", "core", "x", "yl", "z")
CHIPS = ("yh", "x", "yl", "z")
SIZES = (2, 2, 4, 2, 4)
PEERS = 8
ROWS = 2
HALF = 128
MIB = 1 << 20


def device_at(x, y, z, core):
    return int(np.ravel_multi_index((y // 2, core, x, y % 2, z), SIZES))


PLACE = {(0, 0): 0, (1, 0): 1, (1, 1): 2, (0, 1): 3}


def chip(e, f):
    return tuple(PLACE[(e >> k) & 1, (f >> k) & 1] for k in (2, 1, 0))


def device(core, first, second, to=None):
    place = chip(first, second) if core == 0 else chip(second, first)
    return device_at(*place, core if to is None else to)


FIRST = [[device(c, v, s) for v in range(8)] for c in (0, 1) for s in range(8)]
SECOND = [[device(c, s, v) for v in range(8)] for c in (0, 1) for s in range(8)]
ORDER = [
    [ROWS * device(c, first, second) + r for second in range(8) for first in range(8) for r in range(ROWS)]
    for c in (0, 1)
]

def exchange(x, groups):
    return lax.all_to_all(
        x, AXES, split_axis=0, concat_axis=0, axis_index_groups=groups, tiled=True
    )


def swap_cores(x):
    return lax.ppermute(x, "core", [(0, 1), (1, 0)])


def pack_kernel(columns, hidden_ref, ref_ref, out_ref):
    core = lax.axis_index("core")
    for mine in (0, 1):

        @pl.when(core == mine)
        def _(mine=mine):
            for first in range(PEERS):
                target = 0
                for second in range(PEERS):
                    for to in (mine, 1 - mine):
                        source = device(mine, first, second, to) * columns
                        out_ref[first, :, target : target + columns] = ref_ref[:, source : source + columns]
                        target += columns

    rows = hidden_ref[...]
    for peer in range(PEERS):
        out_ref[peer, :, 2 * PEERS * columns :] = rows


def pack(hidden, ref_logprobs, columns):
    width = 2 * PEERS * columns + hidden.shape[1]
    whole = lambda shape: pl.BlockSpec(shape, lambda i: (0,) * len(shape))
    return pl.pallas_call(
        functools.partial(pack_kernel, columns),
        out_shape=jax.ShapeDtypeStruct((PEERS, ROWS, width), hidden.dtype),
        grid=(1,),
        in_specs=[whole(hidden.shape), whole(ref_logprobs.shape)],
        out_specs=whole((PEERS, ROWS, width)),
        compiler_params=pltpu.CompilerParams(vmem_limit_bytes=8 * MIB),
        name="pack",
    )(pltpu.with_memory_space_constraint(hidden, pltpu.HBM), pltpu.with_memory_space_constraint(ref_logprobs, pltpu.HBM))


def spread_kernel(columns, in_ref, rows_ref, lp_ref):
    depth = rows_ref.shape[2]
    first = in_ref.shape[2] - depth

    def rows(start, size):
        parts = [in_ref[peer, :, start : start + size].astype(jnp.float32) for peer in range(PEERS)]
        return jnp.concatenate(parts, axis=0).astype(rows_ref.dtype)

    block = 512
    for start in range(0, depth, block):
        here = rows(first + start, block)
        for peer in range(PEERS):
            rows_ref[peer, :, start : start + block] = here
    for peer in range(PEERS):
        lp_ref[peer] = rows(peer * 2 * columns, 2 * columns)


def spread(got, depth, columns):
    vmem = pl.BlockSpec(memory_space=pltpu.VMEM)
    rows, lp = pl.pallas_call(
        functools.partial(spread_kernel, columns),
        out_shape=(
            jax.ShapeDtypeStruct((PEERS, PEERS * ROWS, depth), got.dtype),
            jax.ShapeDtypeStruct((PEERS, PEERS * ROWS, 2 * columns), got.dtype),
        ),
        in_specs=[vmem],
        out_specs=(vmem, vmem),
        compiler_params=pltpu.CompilerParams(vmem_limit_bytes=8 * MIB),
        name="spread",
    )(got)
    return jnp.concatenate([rows, lp], axis=2)


def token_order(core):
    place = lax.broadcasted_iota(jnp.int32, (1, HALF), 1)
    second, first, row = place >> 4, (place >> 1) & 7, place & 1
    e = jnp.where(core == 0, first, second)
    f = first + second - e
    low = e ^ f
    bit = lambda v, k: (v >> k) & 1
    index = bit(f, 1) * 2 + core
    index = index * 4 + 2 * bit(f, 2) + bit(low, 2)
    index = index * 2 + bit(low, 1)
    index = index * 4 + 2 * bit(f, 0) + bit(low, 0)
    return ROWS * index + row


def token_lines(columns, id_ref, mask_ref, advantage_ref):
    core = lax.axis_index("core")
    mine = lax.axis_index(AXES)
    other = mine + (1 - 2 * core) * (SIZES[2] * SIZES[3] * SIZES[4])
    tokens = id_ref.shape[1]
    lines = [
        id_ref[...].astype(jnp.float32),
        grad_scale * mask_ref[...].astype(jnp.float32),
        advantage_ref[...],
        jnp.zeros((HALF - 3, tokens), jnp.float32),
    ]
    table = jnp.concatenate(lines, axis=0).T
    here = lax.broadcasted_iota(jnp.int32, (tokens, HALF), 0) == token_order(core)
    ids, weighting, advantage = (
        jnp.sum(jnp.where(here, table[:, i : i + 1], 0.0), axis=0, keepdims=True) for i in range(3)
    )
    places = [ids - (d * columns).astype(jnp.float32) for d in (mine, other)]
    return jnp.concatenate(places + [weighting, advantage, jnp.zeros((4, HALF), jnp.float32)], axis=0)


def logits_kernel(
    block, own_ref, weight_ref, other_weight_ref, id_ref, mask_ref, advantage_ref,
    logits_ref, stats_ref, token_ref, rows_ref, sem,
):
    depth, columns = weight_ref.shape
    leave = pltpu.make_async_copy(own_ref.at[:, pl.ds(0, depth)], rows_ref, sem)
    leave.start()
    for side, w_ref in enumerate((weight_ref, other_weight_ref)):
        here = slice(side * columns, (side + 1) * columns)
        for step in range(depth // block):
            rows = slice(step * block, (step + 1) * block)
            part = jnp.dot(own_ref[:, rows], w_ref[rows, :], preferred_element_type=jnp.float32)
            if step == 0:
                logits_ref[:, here] = part
            else:
                logits_ref[:, here] += part
    token_ref[...] = token_lines(columns, id_ref, mask_ref, advantage_ref)
    logits = logits_ref[...]
    top = jnp.max(logits, axis=1, keepdims=True)
    shifted = logits - top
    scaled = jnp.exp(shifted)
    total = jnp.sum(scaled, axis=1, keepdims=True)
    cross = jnp.sum(scaled * (shifted - own_ref[:, depth:].astype(jnp.float32)), axis=1, keepdims=True)
    lane = lax.broadcasted_iota(jnp.int32, (HALF, HALF), 1)
    tile = jnp.where(lane == 0, top, jnp.where(lane == 1, total, cross)).T[:8]
    stats_ref[...] = jnp.broadcast_to(tile[None], stats_ref.shape)
    leave.wait()


def local_logits(own, weight, other_weight, tokens, peers, block=1024):
    depth, columns = weight.shape
    vmem = pl.BlockSpec(memory_space=pltpu.VMEM)
    return pl.pallas_call(
        functools.partial(logits_kernel, block),
        out_shape=(
            jax.ShapeDtypeStruct((HALF, 2 * columns), jnp.float32),
            jax.ShapeDtypeStruct((peers, 8, HALF), jnp.float32),
            jax.ShapeDtypeStruct((8, HALF), jnp.float32),
            pltpu.HBM((HALF, depth), own.dtype),
        ),
        in_specs=[vmem] * 6,
        out_specs=(vmem, vmem, vmem, pl.BlockSpec(memory_space=pltpu.HBM)),
        scratch_shapes=[pltpu.SemaphoreType.DMA],
        compiler_params=pltpu.CompilerParams(vmem_limit_bytes=16 * MIB),
        cost_estimate=pl.CostEstimate(
            flops=4 * HALF * depth * columns, bytes_accessed=4 * depth * columns, transcendentals=0
        ),
        name="logits",
    )(own, weight, other_weight, *(v.reshape(1, -1) for v in tokens))


def hidden_grad_kernel(
    block, logits_ref, own_ref, stats_ref, token_ref, weight_ref, other_weight_ref,
    near_ref, far_ref, out_ref, grad_ref, other_grad_ref, sums, sems,
):
    depth, columns = weight_ref.shape
    steps = depth // block
    tops, totals, crosses = (stats_ref[:, i, :] for i in range(3))
    top = jnp.max(tops, axis=0, keepdims=True)
    below = tops - top
    factor = jnp.exp(below)
    total = jnp.sum(factor * totals, axis=0, keepdims=True)
    cross = jnp.sum(factor * (crosses + below * totals), axis=0, keepdims=True)
    log_total = jnp.log(total)
    divergence = cross / total - log_total
    lines = [top, log_total, divergence, token_ref[0:4, :], jnp.zeros((HALF - 7, HALF), jnp.float32)]
    table = jnp.concatenate(lines, axis=0).T
    row_top, row_log, row_div, place, other_place, weighting, advantage = (table[:, i : i + 1] for i in range(7))
    for side, (g_ref, chosen) in enumerate(((grad_ref, place), (other_grad_ref, other_place))):
        here = slice(side * columns, (side + 1) * columns)
        log_probs = (logits_ref[:, here] - row_top) - row_log
        chance = jnp.exp(log_probs)
        entry = lax.broadcasted_iota(jnp.int32, log_probs.shape, 1).astype(jnp.float32)
        picked = jnp.where(entry == chosen, 1.0, 0.0)
        lp = own_ref[:, depth + side * columns : depth + (side + 1) * columns].astype(jnp.float32)
        grad = weighting * (chance * (log_probs - lp - row_div) - advantage * (picked - chance))
        g_ref[...] = grad.astype(g_ref.dtype)

    def copy(step):
        if step >= steps:
            pair = ((grad_ref, near_ref), (other_grad_ref, far_ref))[step - steps]
            return pltpu.make_async_copy(*pair, sems.at[step])
        here = pl.ds(step * block, block)
        return pltpu.make_async_copy(sums.at[:, here], out_ref.at[:, here], sems.at[step])

    copy(steps).start()
    copy(steps + 1).start()

    for step in range(depth // block):
        here = slice(step * block, (step + 1) * block)
        total = [
            lax.dot_general(w_ref[here, :], g_ref[...], (((1,), (1,)), ((), ())), preferred_element_type=jnp.float32)
            for g_ref, w_ref in ((grad_ref, weight_ref), (other_grad_ref, other_weight_ref))
        ]
        sums[:, here] = (total[0] + total[1]).T.astype(sums.dtype)
        copy(step).start()
    for step in range(steps + 2):
        copy(step).wait()


def hidden_grad(logits, own, stats, token, weight, other_weight, block=1024):
    depth, columns = weight.shape
    part = pltpu.HBM((HALF, columns), weight.dtype)
    return pl.pallas_call(
        functools.partial(hidden_grad_kernel, block),
        out_shape=(part, part, pltpu.HBM((HALF, depth), weight.dtype)),
        in_specs=[pl.BlockSpec(memory_space=pltpu.VMEM)] * 6,
        out_specs=(pl.BlockSpec(memory_space=pltpu.HBM),) * 3,
        scratch_shapes=[
            pltpu.VMEM((HALF, columns), weight.dtype),
            pltpu.VMEM((HALF, columns), weight.dtype),
            pltpu.VMEM((HALF, depth), weight.dtype),
            pltpu.SemaphoreType.DMA((depth // block + 2,)),
        ],
        compiler_params=pltpu.CompilerParams(vmem_limit_bytes=16 * MIB),
        cost_estimate=pl.CostEstimate(
            flops=8 * HALF * depth * columns, bytes_accessed=4 * depth * columns, transcendentals=0
        ),
        name="hidden_grad",
    )(logits, own, stats, token, weight, other_weight)


def total_of(parts):
    parts = [p.astype(jnp.float32) for p in parts]
    while len(parts) > 1:
        parts = [a + b for a, b in zip(parts[::2], parts[1::2])]
    return parts[0]


def sum_kernel(part_ref, out_ref):
    out_ref[...] = total_of([part_ref[peer] for peer in range(PEERS)]).astype(out_ref.dtype)


def add_up(parts):
    vmem = pl.BlockSpec(memory_space=pltpu.VMEM)
    return pl.pallas_call(
        sum_kernel,
        out_shape=jax.ShapeDtypeStruct(parts.shape[1:], parts.dtype),
        in_specs=[vmem],
        out_specs=vmem,
        compiler_params=pltpu.CompilerParams(vmem_limit_bytes=8 * MIB),
        name="add_up",
    )(pltpu.with_memory_space_constraint(parts, pltpu.VMEM))


def head_grad_kernel(own_ref, other_ref, own_grad_ref, other_grad_ref, out_ref):
    x = jnp.concatenate([own_ref[...], other_ref[...]], axis=0)
    grad = jnp.concatenate([own_grad_ref[...], other_grad_ref[...]], axis=0)
    out_ref[...] = lax.dot_general(
        x, grad, (((0,), (0,)), ((), ())), preferred_element_type=jnp.float32
    ).astype(out_ref.dtype)


def head_grad(own, other, own_grad, other_grad, depth, block=1792):
    tokens, columns = own_grad.shape
    x_spec = pl.BlockSpec((HALF, block), lambda k: (0, k))
    grad_spec = pl.BlockSpec(own_grad.shape, lambda k: (0, 0))
    return pl.pallas_call(
        head_grad_kernel,
        out_shape=jax.ShapeDtypeStruct((depth, columns), own_grad.dtype),
        grid=(depth // block,),
        in_specs=[x_spec, x_spec, grad_spec, grad_spec],
        out_specs=pl.BlockSpec((block, columns), lambda k: (k, 0)),
        compiler_params=pltpu.CompilerParams(vmem_limit_bytes=16 * MIB),
        cost_estimate=pl.CostEstimate(
            flops=4 * tokens * depth * columns, bytes_accessed=2 * depth * (columns + 2 * tokens), transcendentals=0
        ),
        name="head_grad",
    )(*(pltpu.with_memory_space_constraint(x, pltpu.HBM) for x in (own, other)), own_grad, other_grad)


def local(hidden, head_weight, ref_logprobs, token_ids, response_mask, advantages):
    depth, columns = head_weight.shape
    other_weight = pltpu.with_memory_space_constraint(swap_cores(head_weight), pltpu.VMEM)
    weight = pltpu.with_memory_space_constraint(head_weight, pltpu.VMEM)

    sent = pack(hidden, ref_logprobs, columns)
    sent = spread(exchange(sent, FIRST), depth, columns)
    own = exchange(sent, SECOND).reshape(HALF, depth + 2 * columns)

    tokens = (token_ids, response_mask, advantages)
    near = pltpu.with_memory_space_constraint(own, pltpu.VMEM)
    logits, stats, token, rows = local_logits(near, weight, other_weight, tokens, 64)
    stats = lax.all_to_all(stats, CHIPS, split_axis=0, concat_axis=0, tiled=True)
    rows, stats = lax.optimization_barrier((rows, stats))
    other = swap_cores(rows)

    grad, theirs, part = hidden_grad(logits, near, stats, token, weight, other_weight)
    grad_head = head_grad(rows, other, grad, swap_cores(theirs), depth)

    part = exchange(part.reshape(PEERS, PEERS * ROWS, depth), SECOND)
    part, grad_head = lax.optimization_barrier((part, grad_head))
    part = add_up(part)
    grad_hidden = add_up(exchange(part.reshape(PEERS, ROWS, depth), FIRST))
    return grad_hidden, grad_head


def solution(mesh):
    fine = Mesh(mesh.devices.reshape(SIZES), AXES)
    return jax.shard_map(
        local,
        mesh=fine,
        in_specs=(P(AXES, None), P(None, AXES), P(AXES, None), P(), P(), P()),
        out_specs=(P(AXES, None), P(None, AXES)),
        check_vma=False,
    )
```
